256 devices in a mesh: section: 16 (over z_lo, y, core), seq: 16 (over x, z_hi).
Axes of the slice: x: 4, y: 4, z: 8 (z_hi: 4, z_lo: 2; z = z_hi * 2 + z_lo), core: 2. Of those that a mesh axis runs over, the one named last changes fastest.
Arguments:
- query: bfloat16 [128, 384, 4096], P('section', 'seq'), may hold values from -5 to 5
- key: bfloat16 [128, 384, 4096], P('section', 'seq'), may hold values from -5 to 5
- value: bfloat16 [128, 384, 4096], P('section', 'seq'), may hold values from -6 to 6
- qk_gain: float32 [2, 4096], replicated, may hold values from 1 to 2
- timesteps: int32 [128], P('section'), may hold values from 0 to 999, as said below
- gate_weight: bfloat16 [256, 4096], replicated, may hold values from -0.375 to 0.375
- slot: int32 [1], replicated, may hold values from 0 to 7
- fresh: bfloat16 [384, 4096], P('seq'), may hold values from -6 to 6
Outputs:
- shifted: bfloat16 [128, 384, 4096], P('section', 'seq')
The draws below stay inside these ranges and needn't reach their ends.
Inputs may be any that keep to these rules, and one draw needn't show every extreme that they name: `timesteps`: never falls along the queue; the first frame has 0 and the last 999.
All inputs are finite; a program needn't handle non-finite values.
Results may differ from the reference program's by a relative error of at most 0.0084.
Values may be sent and summed in bfloat16 or wider, within the bound.
No kernel may reach another device: no remote copies, remote signals or barrier semaphores. Data moves between devices by JAX's collectives and lax.ppermute only.
A program may use at most 256 MiB of HBM per device.

```python
import math
import jax
import jax.numpy as jnp
from jax import lax

HEADS = 32
HD = 128
FREQ_DIM = 256
LEVELS = 1000
F_PART = 8
INNER = 4096
FT = 384
FRAMES = 128
N_SECTION = 16


def draw_query(key, part):
    key = jax.random.fold_in(key, 11)
    drawn = jnp.clip(jax.random.normal(key, (FRAMES, FT, HEADS * HD), jnp.float32), -5.0, 5.0)
    return drawn.astype(jnp.bfloat16)


def draw_key(key, part):
    key = jax.random.fold_in(key, 13)
    drawn = jnp.clip(jax.random.normal(key, (FRAMES, FT, HEADS * HD), jnp.float32), -5.0, 5.0)
    return drawn.astype(jnp.bfloat16)


def draw_timesteps(key, part):
    key = jax.random.fold_in(key, 23)
    spacing = (LEVELS - 1) // FRAMES
    frame = jnp.arange(FRAMES, dtype=jnp.int32)
    jitter = jax.random.randint(key, (FRAMES,), 0, spacing)
    levels = frame * spacing + jitter
    levels = jnp.where(frame == FRAMES - 1, LEVELS - 1, levels)
    levels = jnp.where(frame == 0, 0, levels)
    return levels.astype(jnp.int32)


def level_of(key, dims, pieces, least, largest):
    level, own = 1.0, jax.random.fold_in(key, 6)
    for axis_at, shards_of in pieces:
        draws = jnp.exp(jax.random.uniform(jax.random.fold_in(own, axis_at), (shards_of,), jnp.float32, least / len(pieces), largest / len(pieces)))
        level = level * jnp.repeat(draws, dims[axis_at] // shards_of).reshape([-1 if axis == axis_at else 1 for axis in range(len(dims))])
    return level


def normal_values(rng, extent, deviation, most, cuts=(), held_as=jnp.bfloat16):
    entries = deviation * jax.random.normal(rng, extent, jnp.float32)
    if cuts:
        entries = entries * level_of(rng, extent, cuts, -0.22, 0.18)
    return jnp.clip(entries, -most, most).astype(held_as)


def setup_inputs(seed: int = 0) -> dict:
    streams_of = jax.random.split(jax.random.key(seed), 9)
    return {
        "query": draw_query(jax.random.fold_in(streams_of[8], 71), 0),
        "key": draw_key(jax.random.fold_in(streams_of[8], 71), 0),
        "value": normal_values(streams_of[2], (FRAMES, FT, INNER), 1.0, 6.0, ((0, 16), (1, 16))),
        "qk_gain": jnp.clip(jax.random.uniform(streams_of[3], (2, INNER), jnp.float32, 1.0, 2.0), 1.0, 2.0),
        "timesteps": draw_timesteps(jax.random.fold_in(streams_of[8], 71), 0),
        "gate_weight": normal_values(streams_of[5], (FREQ_DIM, INNER), FREQ_DIM ** -0.5, 0.375),
        "slot": jax.random.randint(streams_of[6], (1,), 0, F_PART).astype(jnp.int32),
        "fresh": normal_values(streams_of[7], (FT, INNER), 1.0, 6.0, ((0, 16),)),
    }


def rms_scaled(values, gain):
    widened = values.astype(jnp.float32)
    factor = lax.rsqrt(lax.optimization_barrier(jnp.mean(widened * widened, axis=-1, keepdims=True)) + 1e-06)
    return (widened * factor * gain).astype(jnp.bfloat16)

def level_gate(steps, gate_weight):
    half = gate_weight.shape[0] // 2
    freqs = jnp.exp(-math.log(10000.0) * jnp.arange(half, dtype=jnp.float32) / half)
    angles = steps.astype(jnp.float32)[:, None] * freqs[None, :]
    embed = jnp.concatenate([jnp.cos(angles), jnp.sin(angles)], axis=1).astype(jnp.bfloat16)
    return jnp.dot(embed, gate_weight, preferred_element_type=jnp.float32)

def one_head(operands):
    queries, keys, values = operands
    scores = jnp.dot(queries, keys.T, preferred_element_type=jnp.float32) * (1.0 / math.sqrt(HD))
    peak = lax.optimization_barrier(jnp.max(scores, axis=1, keepdims=True))
    weights = jnp.exp(scores - peak)
    totals = lax.optimization_barrier(jnp.sum(weights, axis=1, keepdims=True))
    mixed = jnp.dot(weights.astype(jnp.bfloat16), values, preferred_element_type=jnp.float32)
    return (mixed / totals).astype(jnp.bfloat16)

def one_partition(operands):
    queries, keys, values = operands
    return lax.map(one_head, (queries, keys, values))

def reference(query, key, value, qk_gain, timesteps, gate_weight, slot, fresh):
    length = F_PART * FT
    qn = rms_scaled(query, qk_gain[0])
    kn = rms_scaled(key, qk_gain[1])

    def by_heads(array):
        return array.reshape(N_SECTION, length, HEADS, HD).transpose(0, 2, 1, 3)
    attended = lax.map(one_partition, (by_heads(qn), by_heads(kn), by_heads(value)))
    attended = attended.transpose(0, 2, 1, 3).reshape(FRAMES, FT, HEADS * HD)
    gate = level_gate(timesteps, gate_weight)
    gated = (gate[:, None, :] * attended.astype(jnp.float32)).astype(jnp.bfloat16)
    grouped = gated.reshape(N_SECTION, F_PART, FT, HEADS * HD)
    position = slot[0]
    leaving = grouped[:, position]
    arriving = jnp.concatenate([fresh[None], leaving[:-1]], axis=0)
    grouped = grouped.at[:, position].set(arriving)
    return grouped.reshape(FRAMES, FT, HEADS * HD)
```

```python
import math

import jax
import jax.numpy as jnp
from jax import lax
from jax.experimental import pallas as pl
from jax.experimental.pallas import tpu as pltpu
from jax.sharding import PartitionSpec as P

HD = 128
SIDE = 4
LOG2E = 1.4426950408889634
AXES = (("z", "x"), ("x", "z"))
MIB = 1024 * 1024


def moved(value, axis, steps):
    pairs = []
    for source in range(SIDE * SIDE):
        x, z = divmod(source, SIDE)
        if axis == "x":
            x = (x + steps) % SIDE
        else:
            z = (z + steps) % SIDE
        pairs.append((source, x * SIDE + z))
    return lax.ppermute(value, "seq", pairs)


def exchange(pieces, axes, sign):
    first, second = axes
    held = [pieces[0]] + [moved(pieces[i], first, sign * i) for i in range(1, SIDE)]
    arrived = [
        moved(jnp.stack([held[i][j] for i in range(SIDE)]), second, sign * j)
        for j in range(1, SIDE)
    ]
    return held, arrived


def group_of(place, axes, i, j):
    steps = {axes[0]: i, axes[1]: j}
    x = lax.rem(place[0] + steps["x"], SIDE)
    z = lax.rem(place[1] + steps["z"], SIDE)
    return (x * SIDE + z) * (2 * HD)


def prepare_kernel(place, q_ref, k_ref, v_ref, gain_ref, *outs):
    inner = q_ref.shape[2]

    def factor_of(ref):
        total = None
        for at in range(0, inner, 512):
            part = ref[:, :, at : at + 512].astype(jnp.float32)
            part = part * part
            total = part if total is None else total + part
        mean = jnp.sum(total, axis=-1, keepdims=True) * (1.0 / inner)
        return lax.rsqrt(mean + 1e-06)

    q_factor, k_factor = factor_of(q_ref), factor_of(k_ref)
    for head in range(2):
        for i in range(SIDE):
            for j in range(SIDE):
                at = pl.multiple_of(group_of(place, AXES[head], i, j) + head * HD, HD)
                out = outs[head * SIDE + i]
                for kind, (ref, factor) in enumerate(((q_ref, q_factor), (k_ref, k_factor))):
                    gain = gain_ref[kind : kind + 1, pl.ds(at, HD)]
                    part = ref[:, :, pl.ds(at, HD)].astype(jnp.float32) * factor * gain[None]
                    out[j, kind] = part.astype(jnp.bfloat16)
                out[j, 2] = v_ref[:, :, pl.ds(at, HD)]


def prepare(place, query, key, value, qk_gain):
    frames, rows, inner = query.shape
    step = 2
    tall = pl.BlockSpec((step, rows, inner), lambda n, _: (n, 0, 0))
    out = pl.BlockSpec((SIDE, 3, step, rows, HD), lambda n, _: (0, 0, n, 0, 0))
    shape = jax.ShapeDtypeStruct((SIDE, 3, frames, rows, HD), jnp.bfloat16)
    return pl.pallas_call(
        prepare_kernel,
        grid_spec=pltpu.PrefetchScalarGridSpec(
            num_scalar_prefetch=1,
            grid=(frames // step,),
            in_specs=[tall, tall, tall, pl.BlockSpec((2, inner), lambda n, _: (0, 0))],
            out_specs=[out] * (2 * SIDE),
        ),
        out_shape=[shape] * (2 * SIDE),
        compiler_params=pltpu.CompilerParams(vmem_limit_bytes=40 * MIB),
        cost_estimate=pl.CostEstimate(
            flops=10 * query.size, bytes_accessed=12 * query.size, transcendentals=0
        ),
        name="prepare",
    )(place, query, key, value, qk_gain)


def attend_kernel(gate_ref, *refs):
    held, arrived = refs[:SIDE], refs[SIDE : 2 * SIDE - 1]
    outs = refs[2 * SIDE - 1 : 3 * SIDE - 1]
    q_all, k_all, v_all, s_even, s_odd, m_even, m_odd, gates, result = refs[3 * SIDE - 1 :]
    frames, rows = held[0].shape[2:4]
    tokens = frames * rows
    length = SIDE * SIDE * tokens
    block, chunk = 256, 512
    blocks = length // block
    scale = LOG2E / math.sqrt(HD)

    for i in range(SIDE):
        for j in range(SIDE):
            at = (i * SIDE + j) * tokens
            for kind, place in enumerate((q_all, k_all, v_all)):
                part = held[i][0, kind] if j == 0 else arrived[j - 1][i, kind]
                place[at : at + tokens, :HD] = part.reshape(tokens, HD)
    v_all[:, HD:] = jnp.ones((length, HD), jnp.bfloat16)
    for at in range(SIDE * frames):
        gates[at * rows : (at + 1) * rows, :] = jnp.broadcast_to(
            gate_ref[at % frames : at % frames + 1, :], (rows, HD)
        )

    def rows_of(n):
        at = n * block
        return pl.ds(at if isinstance(n, int) else pl.multiple_of(at, block), block)

    def step(following, s_next, m_next, current, s_now, m_now):
        if following is not None:
            q = q_all[rows_of(following), :]
            peak = None
        if current is not None:
            most = m_now[...] * scale
            total = None
        for at in range(0, length, chunk):
            if following is not None:
                scores = lax.dot_general(
                    q,
                    k_all[at : at + chunk, :],
                    (((1,), (1,)), ((), ())),
                    preferred_element_type=jnp.float32,
                )
                s_next[:, at : at + chunk] = scores
                for lane in range(0, chunk, HD):
                    part = scores[:, lane : lane + HD]
                    peak = part if peak is None else jnp.maximum(peak, part)
            if current is not None:
                weights = [
                    jnp.exp2(s_now[:, at + lane : at + lane + HD] * scale - most).astype(jnp.bfloat16)
                    for lane in range(0, chunk, HD)
                ]
                part = jnp.dot(
                    jnp.concatenate(weights, axis=1),
                    v_all[at : at + chunk, :],
                    preferred_element_type=jnp.float32,
                )
                total = part if total is None else total + part
        if following is not None:
            m_next[...] = jnp.broadcast_to(jnp.max(peak, axis=1, keepdims=True), (block, HD))
        if current is not None:
            attended = (total[:, :HD] / total[:, HD:]).astype(jnp.bfloat16).astype(jnp.float32)
            gate = gates[rows_of(current % (SIDE * tokens // block)), :]
            result[rows_of(current), :] = (gate * attended).astype(jnp.bfloat16)

    even, odd = (s_even, m_even), (s_odd, m_odd)
    step(0, *even, None, None, None)

    @pl.loop(0, blocks // 2 - 1)
    def _(pair):
        step(2 * pair + 1, *odd, 2 * pair, *even)
        step(2 * pair + 2, *even, 2 * pair + 1, *odd)

    step(blocks - 1, *odd, blocks - 2, *even)
    step(None, None, None, blocks - 1, *odd)
    for i in range(SIDE):
        for j in range(SIDE):
            at = (i * SIDE + j) * tokens
            outs[i][j] = result[at : at + tokens, :].reshape(frames, rows, HD)


def attend(gate, held, arrived):
    frames, rows = held[0].shape[2:4]
    length = SIDE * SIDE * frames * rows
    block = 256
    one = pl.BlockSpec((1, 3, frames, rows, HD), lambda n: (0, 0, 0, 0, 0))
    whole = pl.BlockSpec((SIDE, 3, frames, rows, HD), lambda n: (0, 0, 0, 0, 0))
    return pl.pallas_call(
        attend_kernel,
        grid=(1,),
        in_specs=[pl.BlockSpec((frames, HD), lambda n: (0, 0))] + [one] * SIDE + [whole] * (SIDE - 1),
        out_specs=[pl.BlockSpec((SIDE, frames, rows, HD), lambda n: (0, 0, 0, 0))] * SIDE,
        out_shape=[jax.ShapeDtypeStruct((SIDE, frames, rows, HD), jnp.bfloat16)] * SIDE,
        scratch_shapes=[
            pltpu.VMEM((length, HD), jnp.bfloat16),
            pltpu.VMEM((length, HD), jnp.bfloat16),
            pltpu.VMEM((length, 2 * HD), jnp.bfloat16),
            pltpu.VMEM((block, length), jnp.float32),
            pltpu.VMEM((block, length), jnp.float32),
            pltpu.VMEM((block, HD), jnp.float32),
            pltpu.VMEM((block, HD), jnp.float32),
            pltpu.VMEM((SIDE * frames * rows, HD), jnp.float32),
            pltpu.VMEM((length, HD), jnp.bfloat16),
        ],
        compiler_params=pltpu.CompilerParams(vmem_limit_bytes=48 * MIB),
        cost_estimate=pl.CostEstimate(
            flops=8 * length * length * HD, bytes_accessed=8 * length * HD, transcendentals=length * length
        ),
        name="attend",
    )(gate, *held, *arrived)


def leaving_kernel(slot, *refs):
    out = refs[-1]
    for i in range(SIDE):
        for j in range(SIDE):
            part = refs[i][0, 0] if j == 0 else refs[SIDE + j - 1][i, 0]
            out[i * SIDE + j] = part


def leaving_frame(slot, held, arrived):
    rows = held[0].shape[2]
    one = pl.BlockSpec((1, 1, rows, HD), lambda n, s: (0, s[0], 0, 0))
    whole = pl.BlockSpec((SIDE, 1, rows, HD), lambda n, s: (0, s[0], 0, 0))
    count = SIDE * SIDE
    return pl.pallas_call(
        leaving_kernel,
        grid_spec=pltpu.PrefetchScalarGridSpec(
            num_scalar_prefetch=1,
            grid=(1,),
            in_specs=[one] * SIDE + [whole] * (SIDE - 1),
            out_specs=pl.BlockSpec((count, rows, HD), lambda n, s: (0, 0, 0)),
        ),
        out_shape=jax.ShapeDtypeStruct((count, rows, HD), jnp.bfloat16),
        name="leaving",
    )(slot, *held, *arrived)


def assemble_kernel(place, *refs):
    fresh, out = refs[-2:]
    per_head = 2 * SIDE
    step = out.shape[0]
    first = pl.program_id(0) * step
    for n in range(step):
        here = first + n == place[2]

        @pl.when(jnp.logical_not(here))
        def _(n=n):
            for head in range(2):
                own = refs[head * per_head : (head + 1) * per_head]
                for i in range(SIDE):
                    for j in range(SIDE):
                        at = pl.multiple_of(group_of(place, AXES[head], i, j) + head * HD, HD)
                        part = own[i][0, n] if j == 0 else own[SIDE + j - 1][i, n]
                        out[n, :, pl.ds(at, HD)] = part

        @pl.when(jnp.logical_and(here, place[3] != 0))
        def _(n=n):
            for head in range(2):
                arriving = refs[(head + 1) * per_head - 1]
                for i in range(SIDE):
                    for j in range(SIDE):
                        at = pl.multiple_of(group_of(place, AXES[head], i, j) + head * HD, HD)
                        out[n, :, pl.ds(at, HD)] = arriving[i * SIDE + j]

        @pl.when(jnp.logical_and(here, place[3] == 0))
        def _(n=n):
            out[n] = fresh[...]


def assemble(place, parts, fresh):
    frames, rows = parts[0][0][0].shape[1:3]
    inner = fresh.shape[1]
    step = 2
    one = pl.BlockSpec((1, step, rows, HD), lambda n, _: (0, n, 0, 0))
    whole = pl.BlockSpec((SIDE, step, rows, HD), lambda n, _: (0, n, 0, 0))
    arriving = pl.BlockSpec((SIDE * SIDE, rows, HD), lambda n, _: (0, 0, 0))
    operands = []
    for held, arrived, behind in parts:
        operands += [*held, *arrived, behind]
    return pl.pallas_call(
        assemble_kernel,
        grid_spec=pltpu.PrefetchScalarGridSpec(
            num_scalar_prefetch=1,
            grid=(frames // step,),
            in_specs=([one] * SIDE + [whole] * (SIDE - 1) + [arriving]) * 2
            + [pl.BlockSpec((rows, inner), lambda n, _: (0, 0))],
            out_specs=pl.BlockSpec((step, rows, inner), lambda n, _: (n, 0, 0)),
        ),
        out_shape=jax.ShapeDtypeStruct((frames, rows, inner), jnp.bfloat16),
        compiler_params=pltpu.CompilerParams(vmem_limit_bytes=40 * MIB),
        name="assemble",
    )(place, *operands, fresh)


def level_gate(steps, gate_weight):
    half = gate_weight.shape[0] // 2
    freqs = jnp.exp(-math.log(10000.0) * jnp.arange(half, dtype=jnp.float32) / half)
    angles = steps.astype(jnp.float32)[:, None] * freqs[None, :]
    embed = jnp.concatenate([jnp.cos(angles), jnp.sin(angles)], axis=1).astype(jnp.bfloat16)
    return jnp.dot(embed, gate_weight, preferred_element_type=jnp.float32)


def shards(query, key, value, qk_gain, timesteps, gate_weight, slot, fresh):
    index = lax.axis_index("seq")
    section = lax.axis_index("section")
    place = jnp.stack([index // SIDE, index % SIDE, slot[0], section]).astype(jnp.int32)
    columns = lax.dynamic_slice_in_dim(gate_weight, index * (2 * HD), 2 * HD, 1)
    gate = level_gate(timesteps, columns)
    prepared = prepare(place, query, key, value, qk_gain)
    sent = [exchange(prepared[head * SIDE : (head + 1) * SIDE], AXES[head], 1) for head in range(2)]
    sections = lax.axis_size("section")
    parts = []
    for head in range(2):
        result = attend(gate[:, head * HD : (head + 1) * HD], *sent[head])
        held, arrived = exchange(result, AXES[head], -1)
        leaving = leaving_frame(slot, held, arrived)
        behind = lax.ppermute(leaving, "section", [(n, n + 1) for n in range(sections - 1)])
        parts.append((held, arrived, behind))
    return assemble(place, parts, fresh)


def solution(mesh):
    placed = (
        P("section", "seq", None),
        P("section", "seq", None),
        P("section", "seq", None),
        P(),
        P("section"),
        P(),
        P(),
        P("seq", None),
    )
    return jax.shard_map(
        shards, mesh=mesh, in_specs=placed, out_specs=P("section", "seq", None), check_vma=False
    )
```

```python
import math

import jax
import jax.numpy as jnp
from jax import lax
from jax.experimental import pallas as pl
from jax.experimental.pallas import tpu as pltpu
from jax.sharding import PartitionSpec as P

HD = 128
LOG2E = 1.4426950408889634
MIB = 1024 * 1024


def exchange(pieces):
    return lax.all_to_all(pieces, "seq", split_axis=0, concat_axis=0, tiled=True)


def prepare_kernel(q_ref, k_ref, v_ref, gain_ref, *outs):
    inner = q_ref.shape[2]

    def factor_of(ref):
        total = None
        for at in range(0, inner, 512):
            part = ref[:, :, at : at + 512].astype(jnp.float32)
            part = part * part
            total = part if total is None else total + part
        mean = jnp.sum(total, axis=-1, keepdims=True) * (1.0 / inner)
        return lax.rsqrt(mean + 1e-06)

    q_factor, k_factor = factor_of(q_ref), factor_of(k_ref)
    for head, out in enumerate(outs):
        for group in range(out.shape[0]):
            at = (group * len(outs) + head) * HD
            for kind, (ref, factor) in enumerate(((q_ref, q_factor), (k_ref, k_factor))):
                gain = gain_ref[kind : kind + 1, at : at + HD]
                part = ref[:, :, at : at + HD].astype(jnp.float32) * factor * gain[None]
                out[group, kind] = part.astype(jnp.bfloat16)
            out[group, 2] = v_ref[:, :, at : at + HD]


def prepare(groups, query, key, value, qk_gain):
    frames, rows, inner = query.shape
    heads = inner // HD // groups
    step = 2
    tall = pl.BlockSpec((step, rows, inner), lambda n: (n, 0, 0))
    out = pl.BlockSpec((groups, 3, step, rows, HD), lambda n: (0, 0, n, 0, 0))
    shape = jax.ShapeDtypeStruct((groups, 3, frames, rows, HD), jnp.bfloat16)
    return pl.pallas_call(
        prepare_kernel,
        grid=(frames // step,),
        in_specs=[tall, tall, tall, pl.BlockSpec((2, inner), lambda n: (0, 0))],
        out_specs=[out] * heads,
        out_shape=[shape] * heads,
        compiler_params=pltpu.CompilerParams(vmem_limit_bytes=60 * MIB),
        cost_estimate=pl.CostEstimate(
            flops=10 * query.size, bytes_accessed=12 * query.size, transcendentals=0
        ),
        name="prepare",
    )(query, key, value, qk_gain)


def attend_kernel(gate_ref, sent, out, q_all, k_all, v_all, s_even, s_odd, m_even, m_odd, gates, result):
    sources, _, frames, rows, _ = sent.shape
    tokens = frames * rows
    length = sources * tokens
    block, chunk = 256, 512
    blocks = length // block
    scale = LOG2E / math.sqrt(HD)
    period = gates.shape[0]

    for source in range(sources):
        at = source * tokens
        for kind, place in enumerate((q_all, k_all, v_all)):
            place[at : at + tokens, :HD] = sent[source, kind].reshape(tokens, HD)
    v_all[:, HD:] = jnp.ones((length, HD), jnp.bfloat16)
    for at in range(period // rows):
        gates[at * rows : (at + 1) * rows, :] = jnp.broadcast_to(
            gate_ref[at % frames : at % frames + 1, :], (rows, HD)
        )

    def rows_of(n):
        at = n * block
        return pl.ds(at if isinstance(n, int) else pl.multiple_of(at, block), block)

    def step(following, s_next, m_next, current, s_now, m_now):
        if following is not None:
            q = q_all[rows_of(following), :]
            peak = None
        if current is not None:
            most = m_now[...] * scale
            total = None
        for at in range(0, length, chunk):
            if following is not None:
                scores = lax.dot_general(
                    q,
                    k_all[at : at + chunk, :],
                    (((1,), (1,)), ((), ())),
                    preferred_element_type=jnp.float32,
                )
                s_next[:, at : at + chunk] = scores
                for lane in range(0, chunk, HD):
                    part = scores[:, lane : lane + HD]
                    peak = part if peak is None else jnp.maximum(peak, part)
            if current is not None:
                weights = [
                    jnp.exp2(s_now[:, at + lane : at + lane + HD] * scale - most).astype(jnp.bfloat16)
                    for lane in range(0, chunk, HD)
                ]
                part = jnp.dot(
                    jnp.concatenate(weights, axis=1),
                    v_all[at : at + chunk, :],
                    preferred_element_type=jnp.float32,
                )
                total = part if total is None else total + part
        if following is not None:
            m_next[...] = jnp.broadcast_to(jnp.max(peak, axis=1, keepdims=True), (block, HD))
        if current is not None:
            attended = (total[:, :HD] / total[:, HD:]).astype(jnp.bfloat16).astype(jnp.float32)
            gate = gates[rows_of(current % (period // block)), :]
            result[rows_of(current), :] = (gate * attended).astype(jnp.bfloat16)

    even, odd = (s_even, m_even), (s_odd, m_odd)
    step(0, *even, None, None, None)

    @pl.loop(0, blocks // 2 - 1)
    def _(pair):
        step(2 * pair + 1, *odd, 2 * pair, *even)
        step(2 * pair + 2, *even, 2 * pair + 1, *odd)

    step(blocks - 1, *odd, blocks - 2, *even)
    step(None, None, None, blocks - 1, *odd)
    for source in range(sources):
        at = source * tokens
        out[source] = result[at : at + tokens, :].reshape(frames, rows, HD)


def attend(gate, sent):
    sources, _, frames, rows, _ = sent.shape
    length = sources * frames * rows
    block = 256
    return pl.pallas_call(
        attend_kernel,
        grid=(1,),
        in_specs=[
            pl.BlockSpec((frames, HD), lambda n: (0, 0)),
            pl.BlockSpec(sent.shape, lambda n: (0, 0, 0, 0, 0)),
        ],
        out_specs=pl.BlockSpec((sources, frames, rows, HD), lambda n: (0, 0, 0, 0)),
        out_shape=jax.ShapeDtypeStruct((sources, frames, rows, HD), jnp.bfloat16),
        scratch_shapes=[
            pltpu.VMEM((length, HD), jnp.bfloat16),
            pltpu.VMEM((length, HD), jnp.bfloat16),
            pltpu.VMEM((length, 2 * HD), jnp.bfloat16),
            pltpu.VMEM((block, length), jnp.float32),
            pltpu.VMEM((block, length), jnp.float32),
            pltpu.VMEM((block, HD), jnp.float32),
            pltpu.VMEM((block, HD), jnp.float32),
            pltpu.VMEM((math.lcm(frames * rows, block), HD), jnp.float32),
            pltpu.VMEM((length, HD), jnp.bfloat16),
        ],
        compiler_params=pltpu.CompilerParams(vmem_limit_bytes=60 * MIB),
        cost_estimate=pl.CostEstimate(
            flops=8 * length * length * HD, bytes_accessed=8 * length * HD, transcendentals=length * length
        ),
        name="attend",
    )(gate, sent)


def leaving_frame(slot, returned):
    return lax.dynamic_index_in_dim(returned, slot[0], 1, keepdims=False)


def assemble_kernel(place, *refs):
    fresh, out = refs[-2:]
    heads = (len(refs) - 2) // 2
    step = out.shape[0]
    first = pl.program_id(0) * step
    for n in range(step):
        here = first + n == place[0]

        @pl.when(jnp.logical_not(here))
        def _(n=n):
            for head in range(heads):
                own = refs[2 * head]
                for group in range(own.shape[0]):
                    at = (group * heads + head) * HD
                    out[n, :, at : at + HD] = own[group, n]

        @pl.when(jnp.logical_and(here, place[1] != 0))
        def _(n=n):
            for head in range(heads):
                behind = refs[2 * head + 1]
                for group in range(behind.shape[0]):
                    at = (group * heads + head) * HD
                    out[n, :, at : at + HD] = behind[group]

        @pl.when(jnp.logical_and(here, place[1] == 0))
        def _(n=n):
            out[n] = fresh[...]


def assemble(place, parts, fresh):
    groups, frames, rows, _ = parts[0][0].shape
    inner = fresh.shape[1]
    step = 2
    own = pl.BlockSpec((groups, step, rows, HD), lambda n, _: (0, n, 0, 0))
    behind = pl.BlockSpec((groups, rows, HD), lambda n, _: (0, 0, 0))
    return pl.pallas_call(
        assemble_kernel,
        grid_spec=pltpu.PrefetchScalarGridSpec(
            num_scalar_prefetch=1,
            grid=(frames // step,),
            in_specs=[own, behind] * len(parts) + [pl.BlockSpec((rows, inner), lambda n, _: (0, 0))],
            out_specs=pl.BlockSpec((step, rows, inner), lambda n, _: (n, 0, 0)),
        ),
        out_shape=jax.ShapeDtypeStruct((frames, rows, inner), jnp.bfloat16),
        compiler_params=pltpu.CompilerParams(vmem_limit_bytes=60 * MIB),
        name="assemble",
    )(place, *[part for pair in parts for part in pair], fresh)


def level_gate(steps, gate_weight):
    half = gate_weight.shape[0] // 2
    freqs = jnp.exp(-math.log(10000.0) * jnp.arange(half, dtype=jnp.float32) / half)
    angles = steps.astype(jnp.float32)[:, None] * freqs[None, :]
    embed = jnp.concatenate([jnp.cos(angles), jnp.sin(angles)], axis=1).astype(jnp.bfloat16)
    return jnp.dot(embed, gate_weight, preferred_element_type=jnp.float32)


def shards(query, key, value, qk_gain, timesteps, gate_weight, slot, fresh):
    index = lax.axis_index("seq")
    groups = lax.axis_size("seq")
    sections = lax.axis_size("section")
    place = jnp.stack([slot[0], lax.axis_index("section")]).astype(jnp.int32)
    width = gate_weight.shape[1] // groups
    gate = level_gate(timesteps, lax.dynamic_slice_in_dim(gate_weight, index * width, width, 1))
    prepared = prepare(groups, query, key, value, qk_gain)
    parts = []
    for head, pieces in enumerate(prepared):
        result = attend(gate[:, head * HD : (head + 1) * HD], exchange(pieces))
        returned = exchange(result)
        leaving = leaving_frame(slot, returned)
        behind = lax.ppermute(leaving, "section", [(n, n + 1) for n in range(sections - 1)])
        parts.append((returned, behind))
    return assemble(place, parts, fresh)


def solution(mesh):
    placed = (
        P("section", "seq", None),
        P("section", "seq", None),
        P("section", "seq", None),
        P(),
        P("section"),
        P(),
        P(),
        P("seq", None),
    )
    return jax.shard_map(
        shards, mesh=mesh, in_specs=placed, out_specs=P("section", "seq", None), check_vma=False
    )
```

```python
import functools
import math

import jax
import jax.numpy as jnp
from jax import lax
from jax.experimental import pallas as pl
from jax.experimental.pallas import tpu as pltpu
from jax.sharding import PartitionSpec as P

HD = 128
SIDE = 4
LOG2E = 1.4426950408889634
AXES = ("z", "x")
MIB = 1024 * 1024


def moved(value, axis, steps):
    pairs = []
    for source in range(SIDE * SIDE):
        x, z = divmod(source, SIDE)
        if axis == "x":
            x = (x + steps) % SIDE
        else:
            z = (z + steps) % SIDE
        pairs.append((source, x * SIDE + z))
    return lax.ppermute(value, "seq", pairs)


def exchange(pieces):
    return lax.all_to_all(pieces, "seq", split_axis=0, concat_axis=0, tiled=True)


def stacked(held):
    return [jnp.stack([piece[j] for piece in held]) for j in range(1, SIDE)]


def second_stage(stacks, axis):
    return [moved(stack, axis, j + 1) for j, stack in enumerate(stacks)]


def after(value, *others):
    return lax.optimization_barrier((value, *others))[0]


def index_of(place, axes, i, j):
    steps = {axes[0]: i, axes[1]: j}
    return lax.rem(place[0] + steps["x"], SIDE) * SIDE + lax.rem(place[1] + steps["z"], SIDE)


def prepare_kernel(place, q_ref, k_ref, v_ref, gain_ref, *outs):
    inner = q_ref.shape[2]

    def factor_of(ref):
        total = None
        for at in range(0, inner, 512):
            part = ref[:, :, at : at + 512].astype(jnp.float32)
            part = part * part
            total = part if total is None else total + part
        mean = jnp.sum(total, axis=-1, keepdims=True) * (1.0 / inner)
        return lax.rsqrt(mean + 1e-06)

    q_factor, k_factor = factor_of(q_ref), factor_of(k_ref)

    def place_into(out, index, at):
        for kind, (ref, factor) in enumerate(((q_ref, q_factor), (k_ref, k_factor))):
            gain = gain_ref[kind : kind + 1, pl.ds(at, HD)]
            part = ref[:, :, pl.ds(at, HD)].astype(jnp.float32) * factor * gain[None]
            out[index, kind] = part.astype(jnp.bfloat16)
        out[index, 2] = v_ref[:, :, pl.ds(at, HD)]

    *first, second = outs
    for i in range(SIDE):
        for j in range(SIDE):
            place_into(first[i], j, pl.multiple_of(index_of(place, AXES, i, j) * (2 * HD), HD))
    for group in range(SIDE * SIDE):
        place_into(second, group, group * 2 * HD + HD)


def prepare(place, query, key, value, qk_gain):
    frames, rows, inner = query.shape
    step = 2
    tall = pl.BlockSpec((step, rows, inner), lambda n, _: (n, 0, 0))
    out = pl.BlockSpec((SIDE, 3, step, rows, HD), lambda n, _: (0, 0, n, 0, 0))
    shape = jax.ShapeDtypeStruct((SIDE, 3, frames, rows, HD), jnp.bfloat16)
    return pl.pallas_call(
        prepare_kernel,
        grid_spec=pltpu.PrefetchScalarGridSpec(
            num_scalar_prefetch=1,
            grid=(frames // step,),
            in_specs=[tall, tall, tall, pl.BlockSpec((2, inner), lambda n, _: (0, 0))],
            out_specs=[out] * SIDE
            + [pl.BlockSpec((SIDE * SIDE, 3, step, rows, HD), lambda n, _: (0, 0, n, 0, 0))],
        ),
        out_shape=[shape] * SIDE
        + [jax.ShapeDtypeStruct((SIDE * SIDE, 3, frames, rows, HD), jnp.bfloat16)],
        compiler_params=pltpu.CompilerParams(vmem_limit_bytes=60 * MIB),
        cost_estimate=pl.CostEstimate(
            flops=10 * query.size, bytes_accessed=12 * query.size, transcendentals=0
        ),
        name="prepare",
    )(place, query, key, value, qk_gain)


def attend_kernel(count, place, gate_ref, _, *refs):
    sent = refs[:count]
    out, q_all, k_all, v_all, s_even, s_odd, m_even, m_odd, gates, result = refs[count:]
    frames, rows = sent[0].shape[2:4]
    tokens = frames * rows
    length = SIDE * SIDE * tokens
    block, chunk = 256, 512
    blocks = length // block
    scale = LOG2E / math.sqrt(HD)

    def part_of(n):
        if count == 1:
            return sent[0], n, n
        i, j = divmod(n, SIDE)
        source = index_of(place, AXES, SIDE - i, SIDE - j)
        return (sent[i], 0, source) if j == 0 else (sent[SIDE + j - 1], i, source)

    for n in range(SIDE * SIDE):
        ref, index, _ = part_of(n)
        for kind, whole in enumerate((q_all, k_all, v_all)):
            whole[n * tokens : (n + 1) * tokens, :HD] = ref[index, kind].reshape(tokens, HD)
    v_all[:, HD:] = jnp.ones((length, HD), jnp.bfloat16)
    for at in range(SIDE * frames):
        gates[at * rows : (at + 1) * rows, :] = jnp.broadcast_to(
            gate_ref[at % frames : at % frames + 1, :], (rows, HD)
        )

    def rows_of(n):
        at = n * block
        return pl.ds(at if isinstance(n, int) else pl.multiple_of(at, block), block)

    def step(following, s_next, m_next, current, s_now, m_now):
        if following is not None:
            q = q_all[rows_of(following), :]
            peak = None
        if current is not None:
            most = m_now[...] * scale
            total = None
        for at in range(0, length, chunk):
            if following is not None:
                scores = lax.dot_general(
                    q,
                    k_all[at : at + chunk, :],
                    (((1,), (1,)), ((), ())),
                    preferred_element_type=jnp.float32,
                )
                s_next[:, at : at + chunk] = scores
                for lane in range(0, chunk, HD):
                    part = scores[:, lane : lane + HD]
                    peak = part if peak is None else jnp.maximum(peak, part)
            if current is not None:
                weights = [
                    jnp.exp2(s_now[:, at + lane : at + lane + HD] * scale - most).astype(jnp.bfloat16)
                    for lane in range(0, chunk, HD)
                ]
                part = jnp.dot(
                    jnp.concatenate(weights, axis=1),
                    v_all[at : at + chunk, :],
                    preferred_element_type=jnp.float32,
                )
                total = part if total is None else total + part
        if following is not None:
            m_next[...] = jnp.broadcast_to(jnp.max(peak, axis=1, keepdims=True), (block, HD))
        if current is not None:
            attended = (total[:, :HD] / total[:, HD:]).astype(jnp.bfloat16).astype(jnp.float32)
            gate = gates[rows_of(current % (SIDE * tokens // block)), :]
            result[rows_of(current), :] = (gate * attended).astype(jnp.bfloat16)

    even, odd = (s_even, m_even), (s_odd, m_odd)
    step(0, *even, None, None, None)

    @pl.loop(0, blocks // 2 - 1)
    def _(pair):
        step(2 * pair + 1, *odd, 2 * pair, *even)
        step(2 * pair + 2, *even, 2 * pair + 1, *odd)

    step(blocks - 1, *odd, blocks - 2, *even)
    step(None, None, None, blocks - 1, *odd)
    for n in range(SIDE * SIDE):
        out[part_of(n)[2]] = result[n * tokens : (n + 1) * tokens, :].reshape(frames, rows, HD)


def attend(place, gate, before, *sent):
    frames, rows = sent[0].shape[2:4]
    length = SIDE * SIDE * frames * rows
    block = 256
    one = pl.BlockSpec((1, 3, frames, rows, HD), lambda n, _: (0, 0, 0, 0, 0))
    whole = pl.BlockSpec((SIDE, 3, frames, rows, HD), lambda n, _: (0, 0, 0, 0, 0))
    every = pl.BlockSpec((SIDE * SIDE, 3, frames, rows, HD), lambda n, _: (0, 0, 0, 0, 0))
    return pl.pallas_call(
        functools.partial(attend_kernel, len(sent)),
        grid_spec=pltpu.PrefetchScalarGridSpec(
            num_scalar_prefetch=1,
            grid=(1,),
            in_specs=[pl.BlockSpec((frames, HD), lambda n, _: (0, 0)), pl.BlockSpec(memory_space=pl.ANY)]
            + ([every] if len(sent) == 1 else [one] * SIDE + [whole] * (SIDE - 1)),
            out_specs=pl.BlockSpec((SIDE * SIDE, frames, rows, HD), lambda n, _: (0, 0, 0, 0)),
            scratch_shapes=[
                pltpu.VMEM((length, HD), jnp.bfloat16),
                pltpu.VMEM((length, HD), jnp.bfloat16),
                pltpu.VMEM((length, 2 * HD), jnp.bfloat16),
                pltpu.VMEM((block, length), jnp.float32),
                pltpu.VMEM((block, length), jnp.float32),
                pltpu.VMEM((block, HD), jnp.float32),
                pltpu.VMEM((block, HD), jnp.float32),
                pltpu.VMEM((SIDE * frames * rows, HD), jnp.float32),
                pltpu.VMEM((length, HD), jnp.bfloat16),
            ],
        ),
        out_shape=jax.ShapeDtypeStruct((SIDE * SIDE, frames, rows, HD), jnp.bfloat16),
        compiler_params=pltpu.CompilerParams(vmem_limit_bytes=60 * MIB),
        cost_estimate=pl.CostEstimate(
            flops=28 * length * length * HD, bytes_accessed=8 * length * HD, transcendentals=length * length
        ),
        name="attend",
    )(place, gate, before, *sent)


def leaving_frame(slot, returned):
    return lax.dynamic_index_in_dim(returned, slot[0], 1, keepdims=False)


def assemble_kernel(*refs):
    *parts, out = refs
    for head, own in enumerate(parts):
        for group in range(own.shape[0]):
            at = (group * len(parts) + head) * HD
            out[:, :, at : at + HD] = own[group]


def assemble(parts):
    groups, frames, rows, _ = parts[0].shape
    inner = groups * len(parts) * HD
    step = 2
    own = pl.BlockSpec((groups, step, rows, HD), lambda n: (0, n, 0, 0))
    return pl.pallas_call(
        assemble_kernel,
        grid=(frames // step,),
        in_specs=[own] * len(parts),
        out_specs=pl.BlockSpec((step, rows, inner), lambda n: (n, 0, 0)),
        out_shape=jax.ShapeDtypeStruct((frames, rows, inner), jnp.bfloat16),
        compiler_params=pltpu.CompilerParams(vmem_limit_bytes=60 * MIB),
        cost_estimate=pl.CostEstimate(flops=0, bytes_accessed=4 * frames * rows * inner, transcendentals=0),
        name="assemble",
    )(*parts)


def hand_kernel(place, *refs):
    *behind, fresh, _, out = refs

    @pl.when(place[3] != 0)
    def _():
        for head, part in enumerate(behind):
            for group in range(part.shape[0]):
                at = (group * len(behind) + head) * HD
                out[0, :, at : at + HD] = part[group]

    @pl.when(place[3] == 0)
    def _():
        out[0] = fresh[...]


def hand_over(place, behind, fresh, gated):
    rows, inner = fresh.shape
    part = pl.BlockSpec(behind[0].shape, lambda n, _: (0, 0, 0))
    return pl.pallas_call(
        hand_kernel,
        grid_spec=pltpu.PrefetchScalarGridSpec(
            num_scalar_prefetch=1,
            grid=(1,),
            in_specs=[part] * len(behind)
            + [pl.BlockSpec((rows, inner), lambda n, _: (0, 0)), pl.BlockSpec(memory_space=pl.ANY)],
            out_specs=pl.BlockSpec((1, rows, inner), lambda n, place: (place[2], 0, 0)),
        ),
        out_shape=jax.ShapeDtypeStruct(gated.shape, gated.dtype),
        input_output_aliases={len(behind) + 2: 0},
        compiler_params=pltpu.CompilerParams(vmem_limit_bytes=60 * MIB),
        name="hand_over",
    )(place, *behind, fresh, gated)


def level_gate(steps, gate_weight):
    half = gate_weight.shape[0] // 2
    freqs = jnp.exp(-math.log(10000.0) * jnp.arange(half, dtype=jnp.float32) / half)
    angles = steps.astype(jnp.float32)[:, None] * freqs[None, :]
    embed = jnp.concatenate([jnp.cos(angles), jnp.sin(angles)], axis=1).astype(jnp.bfloat16)
    return jnp.dot(embed, gate_weight, preferred_element_type=jnp.float32)


def shards(query, key, value, qk_gain, timesteps, gate_weight, slot, fresh):
    index = lax.axis_index("seq")
    section = lax.axis_index("section")
    place = jnp.stack([index // SIDE, index % SIDE, slot[0], section]).astype(jnp.int32)
    columns = lax.dynamic_slice_in_dim(gate_weight, index * (2 * HD), 2 * HD, 1)
    gate = level_gate(timesteps, columns)
    prepared = prepare(place, query, key, value, qk_gain)
    *ahead, direct = prepared
    held = [ahead[0], moved(ahead[1], AXES[0], 1), None, moved(ahead[3], AXES[0], 3)]
    held[2] = moved(ahead[2], AXES[0], 2)
    sent = [*held, *second_stage(stacked(held), AXES[1])]
    direct = [exchange(after(direct, held[1], held[3]))]
    sections = lax.axis_size("section")
    parts, behind, before = [], [], qk_gain
    for head, operands in enumerate((sent, direct)):
        before = attend(place, gate[:, head * HD : (head + 1) * HD], before, *operands)
        returned = exchange(before)
        leaving = leaving_frame(slot, returned)
        behind.append(lax.ppermute(leaving, "section", [(n, n + 1) for n in range(sections - 1)]))
        parts.append(returned)
    return hand_over(place, behind, fresh, assemble(parts))


def solution(mesh):
    placed = (
        P("section", "seq", None),
        P("section", "seq", None),
        P("section", "seq", None),
        P(),
        P("section"),
        P(),
        P(),
        P("seq", None),
    )
    return jax.shard_map(
        shards, mesh=mesh, in_specs=placed, out_specs=P("section", "seq", None), check_vma=False
    )
```

```python
import functools
import math

import jax
import jax.numpy as jnp
from jax import lax
from jax.experimental import pallas as pl
from jax.experimental.pallas import tpu as pltpu
from jax.sharding import PartitionSpec as P

HD = 128
SIDE = 4
LOG2E = 1.4426950408889634
AXES = (("z", "x"), ("x", "z"))
MIB = 1024 * 1024


def moved(value, axis, steps):
    pairs = []
    for source in range(SIDE * SIDE):
        x, z = divmod(source, SIDE)
        if axis == "x":
            x = (x + steps) % SIDE
        else:
            z = (z + steps) % SIDE
        pairs.append((source, x * SIDE + z))
    return lax.ppermute(value, "seq", pairs)


def first_stage(pieces, axis):
    return [pieces[0]] + [moved(pieces[i], axis, i) for i in range(1, SIDE)]


def stacked(held):
    return [jnp.stack([piece[j] for piece in held]) for j in range(1, SIDE)]


def second_stage(stacks, axis):
    return [moved(stack, axis, j + 1) for j, stack in enumerate(stacks)]


def after(value, *others):
    return lax.optimization_barrier((value, *others))[0]


def index_of(place, axes, i, j):
    steps = {axes[0]: i, axes[1]: j}
    return lax.rem(place[0] + steps["x"], SIDE) * SIDE + lax.rem(place[1] + steps["z"], SIDE)


def prepare_kernel(place, q_ref, k_ref, v_ref, gain_ref, *outs):
    inner = q_ref.shape[2]

    def factor_of(ref):
        total = None
        for at in range(0, inner, 512):
            part = ref[:, :, at : at + 512].astype(jnp.float32)
            part = part * part
            total = part if total is None else total + part
        mean = jnp.sum(total, axis=-1, keepdims=True) * (1.0 / inner)
        return lax.rsqrt(mean + 1e-06)

    q_factor, k_factor = factor_of(q_ref), factor_of(k_ref)
    for head in range(2):
        for i in range(SIDE):
            for j in range(SIDE):
                at = pl.multiple_of((index_of(place, AXES[head], i, j) * 2 + head) * HD, HD)
                out = outs[head * SIDE + i]
                for kind, (ref, factor) in enumerate(((q_ref, q_factor), (k_ref, k_factor))):
                    gain = gain_ref[kind : kind + 1, pl.ds(at, HD)]
                    part = ref[:, :, pl.ds(at, HD)].astype(jnp.float32) * factor * gain[None]
                    out[j, kind] = part.astype(jnp.bfloat16)
                out[j, 2] = v_ref[:, :, pl.ds(at, HD)]


def prepare(place, query, key, value, qk_gain):
    frames, rows, inner = query.shape
    step = 2
    tall = pl.BlockSpec((step, rows, inner), lambda n, _: (n, 0, 0))
    out = pl.BlockSpec((SIDE, 3, step, rows, HD), lambda n, _: (0, 0, n, 0, 0))
    shape = jax.ShapeDtypeStruct((SIDE, 3, frames, rows, HD), jnp.bfloat16)
    return pl.pallas_call(
        prepare_kernel,
        grid_spec=pltpu.PrefetchScalarGridSpec(
            num_scalar_prefetch=1,
            grid=(frames // step,),
            in_specs=[tall, tall, tall, pl.BlockSpec((2, inner), lambda n, _: (0, 0))],
            out_specs=[out] * (2 * SIDE),
        ),
        out_shape=[shape] * (2 * SIDE),
        compiler_params=pltpu.CompilerParams(vmem_limit_bytes=60 * MIB),
        cost_estimate=pl.CostEstimate(
            flops=10 * query.size, bytes_accessed=12 * query.size, transcendentals=0
        ),
        name="prepare",
    )(place, query, key, value, qk_gain)


def attend_kernel(axes, place, gate_ref, _, *refs):
    held, arrived = refs[:SIDE], refs[SIDE : 2 * SIDE - 1]
    out, q_all, k_all, v_all, s_even, s_odd, m_even, m_odd, gates, result = refs[2 * SIDE - 1 :]
    frames, rows = held[0].shape[2:4]
    tokens = frames * rows
    length = SIDE * SIDE * tokens
    block, chunk = 256, 512
    blocks = length // block
    scale = LOG2E / math.sqrt(HD)

    for i in range(SIDE):
        for j in range(SIDE):
            at = (i * SIDE + j) * tokens
            for kind, whole in enumerate((q_all, k_all, v_all)):
                part = held[i][0, kind] if j == 0 else arrived[j - 1][i, kind]
                whole[at : at + tokens, :HD] = part.reshape(tokens, HD)
    v_all[:, HD:] = jnp.ones((length, HD), jnp.bfloat16)
    for at in range(SIDE * frames):
        gates[at * rows : (at + 1) * rows, :] = jnp.broadcast_to(
            gate_ref[at % frames : at % frames + 1, :], (rows, HD)
        )

    def rows_of(n):
        at = n * block
        return pl.ds(at if isinstance(n, int) else pl.multiple_of(at, block), block)

    def step(following, s_next, m_next, current, s_now, m_now):
        if following is not None:
            q = q_all[rows_of(following), :]
            peak = None
        if current is not None:
            most = m_now[...] * scale
            total = None
        for at in range(0, length, chunk):
            if following is not None:
                scores = lax.dot_general(
                    q,
                    k_all[at : at + chunk, :],
                    (((1,), (1,)), ((), ())),
                    preferred_element_type=jnp.float32,
                )
                s_next[:, at : at + chunk] = scores
                for lane in range(0, chunk, HD):
                    part = scores[:, lane : lane + HD]
                    peak = part if peak is None else jnp.maximum(peak, part)
            if current is not None:
                weights = [
                    jnp.exp2(s_now[:, at + lane : at + lane + HD] * scale - most).astype(jnp.bfloat16)
                    for lane in range(0, chunk, HD)
                ]
                part = jnp.dot(
                    jnp.concatenate(weights, axis=1),
                    v_all[at : at + chunk, :],
                    preferred_element_type=jnp.float32,
                )
                total = part if total is None else total + part
        if following is not None:
            m_next[...] = jnp.broadcast_to(jnp.max(peak, axis=1, keepdims=True), (block, HD))
        if current is not None:
            attended = (total[:, :HD] / total[:, HD:]).astype(jnp.bfloat16).astype(jnp.float32)
            gate = gates[rows_of(current % (SIDE * tokens // block)), :]
            result[rows_of(current), :] = (gate * attended).astype(jnp.bfloat16)

    even, odd = (s_even, m_even), (s_odd, m_odd)
    step(0, *even, None, None, None)

    @pl.loop(0, blocks // 2 - 1)
    def _(pair):
        step(2 * pair + 1, *odd, 2 * pair, *even)
        step(2 * pair + 2, *even, 2 * pair + 1, *odd)

    step(blocks - 1, *odd, blocks - 2, *even)
    step(None, None, None, blocks - 1, *odd)
    for i in range(SIDE):
        for j in range(SIDE):
            at = (i * SIDE + j) * tokens
            source = index_of(place, axes, SIDE - i, SIDE - j)
            out[source] = result[at : at + tokens, :].reshape(frames, rows, HD)


def attend(axes, place, gate, before, held, arrived):
    frames, rows = held[0].shape[2:4]
    length = SIDE * SIDE * frames * rows
    block = 256
    one = pl.BlockSpec((1, 3, frames, rows, HD), lambda n, _: (0, 0, 0, 0, 0))
    whole = pl.BlockSpec((SIDE, 3, frames, rows, HD), lambda n, _: (0, 0, 0, 0, 0))
    return pl.pallas_call(
        functools.partial(attend_kernel, axes),
        grid_spec=pltpu.PrefetchScalarGridSpec(
            num_scalar_prefetch=1,
            grid=(1,),
            in_specs=[pl.BlockSpec((frames, HD), lambda n, _: (0, 0)), pl.BlockSpec(memory_space=pl.ANY)]
            + [one] * SIDE
            + [whole] * (SIDE - 1),
            out_specs=pl.BlockSpec((SIDE * SIDE, frames, rows, HD), lambda n, _: (0, 0, 0, 0)),
            scratch_shapes=[
                pltpu.VMEM((length, HD), jnp.bfloat16),
                pltpu.VMEM((length, HD), jnp.bfloat16),
                pltpu.VMEM((length, 2 * HD), jnp.bfloat16),
                pltpu.VMEM((block, length), jnp.float32),
                pltpu.VMEM((block, length), jnp.float32),
                pltpu.VMEM((block, HD), jnp.float32),
                pltpu.VMEM((block, HD), jnp.float32),
                pltpu.VMEM((SIDE * frames * rows, HD), jnp.float32),
                pltpu.VMEM((length, HD), jnp.bfloat16),
            ],
        ),
        out_shape=jax.ShapeDtypeStruct((SIDE * SIDE, frames, rows, HD), jnp.bfloat16),
        compiler_params=pltpu.CompilerParams(vmem_limit_bytes=60 * MIB),
        cost_estimate=pl.CostEstimate(
            flops=int(0.1 * length * length * HD) if axes[0] == "z" else 28 * length * length * HD, bytes_accessed=length if axes[0] == "z" else 8 * length * HD, transcendentals=0
        ),
        name="attend",
    )(place, gate, before, *held, *arrived)


def leaving_frame(slot, returned):
    return lax.dynamic_index_in_dim(returned, slot[0], 1, keepdims=False)


def assemble_kernel(*refs):
    *parts, out = refs
    for head, own in enumerate(parts):
        for group in range(own.shape[0]):
            at = (group * len(parts) + head) * HD
            out[:, :, at : at + HD] = own[group]


def assemble(parts):
    groups, frames, rows, _ = parts[0].shape
    inner = groups * len(parts) * HD
    step = 2
    own = pl.BlockSpec((groups, step, rows, HD), lambda n: (0, n, 0, 0))
    return pl.pallas_call(
        assemble_kernel,
        grid=(frames // step,),
        in_specs=[own] * len(parts),
        out_specs=pl.BlockSpec((step, rows, inner), lambda n: (n, 0, 0)),
        out_shape=jax.ShapeDtypeStruct((frames, rows, inner), jnp.bfloat16),
        compiler_params=pltpu.CompilerParams(vmem_limit_bytes=60 * MIB),
        cost_estimate=pl.CostEstimate(flops=0, bytes_accessed=4 * frames * rows * inner, transcendentals=0),
        name="assemble",
    )(*parts)


def hand_kernel(place, *refs):
    *behind, fresh, _, out = refs

    @pl.when(place[3] != 0)
    def _():
        for head, part in enumerate(behind):
            for group in range(part.shape[0]):
                at = (group * len(behind) + head) * HD
                out[0, :, at : at + HD] = part[group]

    @pl.when(place[3] == 0)
    def _():
        out[0] = fresh[...]


def hand_over(place, behind, fresh, gated):
    rows, inner = fresh.shape
    part = pl.BlockSpec(behind[0].shape, lambda n, _: (0, 0, 0))
    return pl.pallas_call(
        hand_kernel,
        grid_spec=pltpu.PrefetchScalarGridSpec(
            num_scalar_prefetch=1,
            grid=(1,),
            in_specs=[part] * len(behind)
            + [pl.BlockSpec((rows, inner), lambda n, _: (0, 0)), pl.BlockSpec(memory_space=pl.ANY)],
            out_specs=pl.BlockSpec((1, rows, inner), lambda n, place: (place[2], 0, 0)),
        ),
        out_shape=jax.ShapeDtypeStruct(gated.shape, gated.dtype),
        input_output_aliases={len(behind) + 2: 0},
        compiler_params=pltpu.CompilerParams(vmem_limit_bytes=60 * MIB),
        name="hand_over",
    )(place, *behind, fresh, gated)


def level_gate(steps, gate_weight):
    half = gate_weight.shape[0] // 2
    freqs = jnp.exp(-math.log(10000.0) * jnp.arange(half, dtype=jnp.float32) / half)
    angles = steps.astype(jnp.float32)[:, None] * freqs[None, :]
    embed = jnp.concatenate([jnp.cos(angles), jnp.sin(angles)], axis=1).astype(jnp.bfloat16)
    return jnp.dot(embed, gate_weight, preferred_element_type=jnp.float32)


def shards(query, key, value, qk_gain, timesteps, gate_weight, slot, fresh):
    index = lax.axis_index("seq")
    section = lax.axis_index("section")
    place = jnp.stack([index // SIDE, index % SIDE, slot[0], section]).astype(jnp.int32)
    columns = lax.dynamic_slice_in_dim(gate_weight, index * (2 * HD), 2 * HD, 1)
    gate = level_gate(timesteps, columns)
    prepared = prepare(place, query, key, value, qk_gain)
    ahead, back = list(prepared[:SIDE]), list(prepared[SIDE:])
    held = [None, first_stage(back, AXES[1][0])]
    ahead[2] = after(ahead[2], held[1][2])
    held[0] = first_stage(ahead, AXES[0][0])
    back_stacks = stacked(held[1])
    held[0][2] = after(held[0][2], *back_stacks)
    stacks = [stacked(held[0]), back_stacks]
    sections = lax.axis_size("section")
    parts, behind, before = [], [], qk_gain
    for head in range(2):
        arrived = second_stage(stacks[head], AXES[head][1])
        result = attend(AXES[head], place, gate[:, head * HD : (head + 1) * HD], before, held[head], arrived)
        before = result
        returned = lax.all_to_all(result, "seq", split_axis=0, concat_axis=0, tiled=True)
        leaving = leaving_frame(slot, returned)
        behind.append(lax.ppermute(leaving, "section", [(n, n + 1) for n in range(sections - 1)]))
        parts.append(returned)
    return hand_over(place, behind, fresh, assemble(parts))


def solution(mesh):
    placed = (
        P("section", "seq", None),
        P("section", "seq", None),
        P("section", "seq", None),
        P(),
        P("section"),
        P(),
        P(),
        P("seq", None),
    )
    return jax.shard_map(
        shards, mesh=mesh, in_specs=placed, out_specs=P("section", "seq", None), check_vma=False
    )
```

```python
import functools
import math

import jax
import jax.numpy as jnp
from jax import lax
from jax.experimental import pallas as pl
from jax.experimental.pallas import tpu as pltpu
from jax.sharding import PartitionSpec as P

HD = 128
SIDE = 4
LOG2E = 1.4426950408889634
MIB = 1024 * 1024
ATTEND_MIB = 30


def moved(value, axis, steps):
    pairs = []
    for source in range(SIDE * SIDE):
        x, z = divmod(source, SIDE)
        if axis == "x":
            x = (x + steps) % SIDE
        else:
            z = (z + steps) % SIDE
        pairs.append((source, x * SIDE + z))
    return lax.ppermute(value, "seq", pairs)


def exchange(pieces, **groups):
    return lax.all_to_all(pieces, "seq", split_axis=0, concat_axis=0, tiled=True, **groups)


def first_stage(pieces, axis):
    return [pieces[0]] + [moved(pieces[i], axis, i) for i in range(1, SIDE)]


def stacked(held):
    return [jnp.stack([piece[j] for piece in held]) for j in range(1, SIDE)]


def second_stage(stacks, axis):
    return [moved(stack, axis, j + 1) for j, stack in enumerate(stacks)]


def after(value, *others):
    return lax.optimization_barrier((value, *others))[0]


def index_of(place, axes, i, j):
    steps = {axes[0]: i, axes[1]: j}
    return lax.rem(place[0] + steps["x"], SIDE) * SIDE + lax.rem(place[1] + steps["z"], SIDE)


def prepare_kernel(place, q_ref, k_ref, v_ref, gain_ref, *outs):
    inner = q_ref.shape[2]

    def factor_of(ref):
        total = None
        for at in range(0, inner, 512):
            part = ref[:, :, at : at + 512].astype(jnp.float32)
            part = part * part
            total = part if total is None else total + part
        mean = jnp.sum(total, axis=-1, keepdims=True) * (1.0 / inner)
        return lax.rsqrt(mean + 1e-06)

    q_factor, k_factor = factor_of(q_ref), factor_of(k_ref)
    for head in range(2):
        for i in range(SIDE):
            for j in range(SIDE):
                group = index_of(place, ("z", "x"), i, j)
                if head:
                    group = lax.rem(place[0] + i, SIDE) * SIDE + j
                at = pl.multiple_of((group * 2 + head) * HD, HD)
                out = outs[head * SIDE + i]
                for kind, (ref, factor) in enumerate(((q_ref, q_factor), (k_ref, k_factor))):
                    gain = gain_ref[kind : kind + 1, pl.ds(at, HD)]
                    part = ref[:, :, pl.ds(at, HD)].astype(jnp.float32) * factor * gain[None]
                    out[j, kind] = part.astype(jnp.bfloat16)
                out[j, 2] = v_ref[:, :, pl.ds(at, HD)]


def prepare(place, query, key, value, qk_gain):
    frames, rows, inner = query.shape
    step = 2
    tall = pl.BlockSpec((step, rows, inner), lambda n, _: (n, 0, 0))
    out = pl.BlockSpec((SIDE, 3, step, rows, HD), lambda n, _: (0, 0, n, 0, 0))
    shape = jax.ShapeDtypeStruct((SIDE, 3, frames, rows, HD), jnp.bfloat16)
    return pl.pallas_call(
        prepare_kernel,
        grid_spec=pltpu.PrefetchScalarGridSpec(
            num_scalar_prefetch=1,
            grid=(frames // step,),
            in_specs=[tall, tall, tall, pl.BlockSpec((2, inner), lambda n, _: (0, 0))],
            out_specs=[out] * (2 * SIDE),
        ),
        out_shape=[shape] * (2 * SIDE),
        compiler_params=pltpu.CompilerParams(vmem_limit_bytes=60 * MIB),
        cost_estimate=pl.CostEstimate(
            flops=10 * query.size, bytes_accessed=12 * query.size, transcendentals=0
        ),
        name="prepare",
    )(place, query, key, value, qk_gain)


def attend_kernel(count, place, gate_ref, _, *refs):
    sent = refs[:count]
    out, q_all, k_all, v_all, s_even, s_odd, m_even, m_odd, gates, result = refs[count:]
    frames, rows = sent[0].shape[-3:-1]
    tokens = frames * rows
    length = SIDE * SIDE * tokens
    block, chunk = 256, 512
    blocks = length // block
    scale = LOG2E / math.sqrt(HD)

    def part_of(n):
        i, j = divmod(n, SIDE)
        if count == 1:
            return sent[0], (i, j), lax.rem(place[0] + SIDE - j, SIDE) * SIDE + i
        source = index_of(place, ("z", "x"), SIDE - i, SIDE - j)
        return (sent[i], (0,), source) if j == 0 else (sent[SIDE + j - 1], (i,), source)

    for n in range(SIDE * SIDE):
        ref, index, _ = part_of(n)
        for kind, whole in enumerate((q_all, k_all, v_all)):
            whole[n * tokens : (n + 1) * tokens, :HD] = ref[(*index, kind)].reshape(tokens, HD)
    v_all[:, HD:] = jnp.ones((length, HD), jnp.bfloat16)
    for at in range(SIDE * frames):
        gates[at * rows : (at + 1) * rows, :] = jnp.broadcast_to(
            gate_ref[at % frames : at % frames + 1, :], (rows, HD)
        )

    def rows_of(n):
        at = n * block
        return pl.ds(at if isinstance(n, int) else pl.multiple_of(at, block), block)

    def step(following, s_next, m_next, current, s_now, m_now):
        if following is not None:
            q = q_all[rows_of(following), :]
            peak = None
        if current is not None:
            most = m_now[...] * scale
            total = None
        for at in range(0, length, chunk):
            if following is not None:
                scores = lax.dot_general(
                    q,
                    k_all[at : at + chunk, :],
                    (((1,), (1,)), ((), ())),
                    preferred_element_type=jnp.float32,
                )
                s_next[:, at : at + chunk] = scores
                for lane in range(0, chunk, HD):
                    part = scores[:, lane : lane + HD]
                    peak = part if peak is None else jnp.maximum(peak, part)
            if current is not None:
                weights = [
                    jnp.exp2(s_now[:, at + lane : at + lane + HD] * scale - most).astype(jnp.bfloat16)
                    for lane in range(0, chunk, HD)
                ]
                part = jnp.dot(
                    jnp.concatenate(weights, axis=1),
                    v_all[at : at + chunk, :],
                    preferred_element_type=jnp.float32,
                )
                total = part if total is None else total + part
        if following is not None:
            m_next[...] = jnp.broadcast_to(jnp.max(peak, axis=1, keepdims=True), (block, HD))
        if current is not None:
            attended = (total[:, :HD] / total[:, HD:]).astype(jnp.bfloat16).astype(jnp.float32)
            gate = gates[rows_of(current % (SIDE * tokens // block)), :]
            result[rows_of(current), :] = (gate * attended).astype(jnp.bfloat16)

    even, odd = (s_even, m_even), (s_odd, m_odd)
    step(0, *even, None, None, None)

    @pl.loop(0, blocks // 2 - 1)
    def _(pair):
        step(2 * pair + 1, *odd, 2 * pair, *even)
        step(2 * pair + 2, *even, 2 * pair + 1, *odd)

    step(blocks - 1, *odd, blocks - 2, *even)
    step(None, None, None, blocks - 1, *odd)
    for n in range(SIDE * SIDE):
        out[part_of(n)[2]] = result[n * tokens : (n + 1) * tokens, :].reshape(frames, rows, HD)


def attend(place, gate, before, *sent):
    frames, rows = sent[0].shape[-3:-1]
    length = SIDE * SIDE * frames * rows
    block = 256
    one = pl.BlockSpec((1, 3, frames, rows, HD), lambda n, _: (0, 0, 0, 0, 0))
    whole = pl.BlockSpec((SIDE, 3, frames, rows, HD), lambda n, _: (0, 0, 0, 0, 0))
    every = pl.BlockSpec((SIDE, SIDE, 3, frames, rows, HD), lambda n, _: (0, 0, 0, 0, 0, 0))
    return pl.pallas_call(
        functools.partial(attend_kernel, len(sent)),
        grid_spec=pltpu.PrefetchScalarGridSpec(
            num_scalar_prefetch=1,
            grid=(1,),
            in_specs=[pl.BlockSpec((frames, HD), lambda n, _: (0, 0)), pl.BlockSpec(memory_space=pl.ANY)]
            + ([every] if len(sent) == 1 else [one] * SIDE + [whole] * (SIDE - 1)),
            out_specs=pl.BlockSpec((SIDE * SIDE, frames, rows, HD), lambda n, _: (0, 0, 0, 0)),
            scratch_shapes=[
                pltpu.VMEM((length, HD), jnp.bfloat16),
                pltpu.VMEM((length, HD), jnp.bfloat16),
                pltpu.VMEM((length, 2 * HD), jnp.bfloat16),
                pltpu.VMEM((block, length), jnp.float32),
                pltpu.VMEM((block, length), jnp.float32),
                pltpu.VMEM((block, HD), jnp.float32),
                pltpu.VMEM((block, HD), jnp.float32),
                pltpu.VMEM((SIDE * frames * rows, HD), jnp.float32),
                pltpu.VMEM((length, HD), jnp.bfloat16),
            ],
        ),
        out_shape=jax.ShapeDtypeStruct((SIDE * SIDE, frames, rows, HD), jnp.bfloat16),
        compiler_params=pltpu.CompilerParams(vmem_limit_bytes=ATTEND_MIB * MIB),
        cost_estimate=pl.CostEstimate(
            flops=int(17 * length * length * HD) if len(sent) > 1 else 28 * length * length * HD, bytes_accessed=length if len(sent) > 1 else 8 * length * HD, transcendentals=0
        ),
        name="attend",
    )(place, gate, before, *sent)


def leaving_frame(slot, returned):
    return lax.dynamic_index_in_dim(returned, slot[0], 1, keepdims=False)


def assemble_kernel(*refs):
    *parts, out = refs
    for head, own in enumerate(parts):
        for group in range(own.shape[0]):
            at = (group * len(parts) + head) * HD
            out[:, :, at : at + HD] = own[group]


def assemble(parts):
    groups, frames, rows, _ = parts[0].shape
    inner = groups * len(parts) * HD
    step = 2
    own = pl.BlockSpec((groups, step, rows, HD), lambda n: (0, n, 0, 0))
    return pl.pallas_call(
        assemble_kernel,
        grid=(frames // step,),
        in_specs=[own] * len(parts),
        out_specs=pl.BlockSpec((step, rows, inner), lambda n: (n, 0, 0)),
        out_shape=jax.ShapeDtypeStruct((frames, rows, inner), jnp.bfloat16),
        compiler_params=pltpu.CompilerParams(vmem_limit_bytes=60 * MIB),
        cost_estimate=pl.CostEstimate(flops=0, bytes_accessed=4 * frames * rows * inner, transcendentals=0),
        name="assemble",
    )(*parts)


def hand_kernel(ends, *refs):
    *behind, fresh, _, out = refs

    @pl.when(ends[1] != 0)
    def _():
        for head, part in enumerate(behind):
            for group in range(part.shape[0]):
                at = (group * len(behind) + head) * HD
                out[0, :, at : at + HD] = part[group]

    @pl.when(ends[1] == 0)
    def _():
        out[0] = fresh[...]


def hand_over(ends, behind, fresh, gated):
    rows, inner = fresh.shape
    part = pl.BlockSpec(behind[0].shape, lambda n, _: (0, 0, 0))
    return pl.pallas_call(
        hand_kernel,
        grid_spec=pltpu.PrefetchScalarGridSpec(
            num_scalar_prefetch=1,
            grid=(1,),
            in_specs=[part] * len(behind)
            + [pl.BlockSpec((rows, inner), lambda n, _: (0, 0)), pl.BlockSpec(memory_space=pl.ANY)],
            out_specs=pl.BlockSpec((1, rows, inner), lambda n, ends: (ends[0], 0, 0)),
        ),
        out_shape=jax.ShapeDtypeStruct(gated.shape, gated.dtype),
        input_output_aliases={len(behind) + 2: 0},
        compiler_params=pltpu.CompilerParams(vmem_limit_bytes=60 * MIB),
        name="hand_over",
    )(ends, *behind, fresh, gated)


def level_gate(steps, gate_weight):
    half = gate_weight.shape[0] // 2
    freqs = jnp.exp(-math.log(10000.0) * jnp.arange(half, dtype=jnp.float32) / half)
    angles = steps.astype(jnp.float32)[:, None] * freqs[None, :]
    embed = jnp.concatenate([jnp.cos(angles), jnp.sin(angles)], axis=1).astype(jnp.bfloat16)
    return jnp.dot(embed, gate_weight, preferred_element_type=jnp.float32)


def shards(query, key, value, qk_gain, timesteps, gate_weight, slot, fresh):
    index = lax.axis_index("seq")
    section = lax.axis_index("section")
    place = jnp.stack([index // SIDE, index % SIDE]).astype(jnp.int32)
    ends = jnp.stack([slot[0], section]).astype(jnp.int32)
    columns = lax.dynamic_slice_in_dim(gate_weight, index * (2 * HD), 2 * HD, 1)
    gate = level_gate(timesteps, columns)
    prepared = prepare(place, query, key, value, qk_gain)
    ahead, back = list(prepared[:SIDE]), list(prepared[SIDE:])
    back = first_stage(back, "x")
    ahead[2] = after(ahead[2], back[2])
    ahead = first_stage(ahead, "z")
    columns_of_z = [[x * SIDE + z for z in range(SIDE)] for x in range(SIDE)]
    back[3] = after(back[3], ahead[1], ahead[3])
    direct = exchange(jnp.stack(back, axis=1), axis_index_groups=columns_of_z)
    sent = [*ahead, *second_stage(stacked(ahead), "x")]
    sections = lax.axis_size("section")
    parts, behind, before = [], [], qk_gain
    for head, operands in enumerate((sent, [direct])):
        before = attend(place, gate[:, head * HD : (head + 1) * HD], before, *operands)
        returned = exchange(before)
        leaving = leaving_frame(slot, returned)
        behind.append(lax.ppermute(leaving, "section", [(n, n + 1) for n in range(sections - 1)]))
        parts.append(returned)
    return hand_over(ends, behind, fresh, assemble(parts))


def solution(mesh):
    placed = (
        P("section", "seq", None),
        P("section", "seq", None),
        P("section", "seq", None),
        P(),
        P("section"),
        P(),
        P(),
        P("seq", None),
    )
    return jax.shard_map(
        shards, mesh=mesh, in_specs=placed, out_specs=P("section", "seq", None), check_vma=False
    )
```

```python
import functools
import math

import jax
import jax.numpy as jnp
from jax import lax
from jax.experimental import pallas as pl
from jax.experimental.pallas import tpu as pltpu
from jax.sharding import PartitionSpec as P

HD = 128
SIDE = 4
LOG2E = 1.4426950408889634
AXES = (("z", "x"), ("x", "z"))
MIB = 1024 * 1024
BLOCK = 512


def moved(value, axis, steps):
    pairs = []
    for source in range(SIDE * SIDE):
        x, z = divmod(source, SIDE)
        if axis == "x":
            x = (x + steps) % SIDE
        else:
            z = (z + steps) % SIDE
        pairs.append((source, x * SIDE + z))
    return lax.ppermute(value, "seq", pairs)


def first_stage(pieces, axis):
    return [pieces[0]] + [moved(pieces[i], axis, i) for i in range(1, SIDE)]


def stacked(held):
    return [jnp.stack([piece[j] for piece in held]) for j in range(1, SIDE)]


def second_stage(stacks, axis):
    return [moved(stack, axis, j + 1) for j, stack in enumerate(stacks)]


def after(value, *others):
    return lax.optimization_barrier((value, *others))[0]


def index_of(place, axes, i, j):
    steps = {axes[0]: i, axes[1]: j}
    return lax.rem(place[0] + steps["x"], SIDE) * SIDE + lax.rem(place[1] + steps["z"], SIDE)


def prepare_kernel(place, q_ref, k_ref, v_ref, gain_ref, *outs):
    inner = q_ref.shape[2]

    def factor_of(ref):
        total = None
        for at in range(0, inner, 512):
            part = ref[:, :, at : at + 512].astype(jnp.float32)
            part = part * part
            total = part if total is None else total + part
        mean = jnp.sum(total, axis=-1, keepdims=True) * (1.0 / inner)
        return lax.rsqrt(mean + 1e-06)

    q_factor, k_factor = factor_of(q_ref), factor_of(k_ref)
    for head in range(2):
        for i in range(SIDE):
            for j in range(SIDE):
                at = pl.multiple_of((index_of(place, AXES[head], i, j) * 2 + head) * HD, HD)
                out = outs[head * SIDE + i]
                for kind, (ref, factor) in enumerate(((q_ref, q_factor), (k_ref, k_factor))):
                    gain = gain_ref[kind : kind + 1, pl.ds(at, HD)]
                    part = ref[:, :, pl.ds(at, HD)].astype(jnp.float32) * factor * gain[None]
                    out[j, kind] = part.astype(jnp.bfloat16)
                out[j, 2] = v_ref[:, :, pl.ds(at, HD)]


def prepare(place, query, key, value, qk_gain):
    frames, rows, inner = query.shape
    step = 2
    tall = pl.BlockSpec((step, rows, inner), lambda n, _: (n, 0, 0))
    out = pl.BlockSpec((SIDE, 3, step, rows, HD), lambda n, _: (0, 0, n, 0, 0))
    shape = jax.ShapeDtypeStruct((SIDE, 3, frames, rows, HD), jnp.bfloat16)
    return pl.pallas_call(
        prepare_kernel,
        grid_spec=pltpu.PrefetchScalarGridSpec(
            num_scalar_prefetch=1,
            grid=(frames // step,),
            in_specs=[tall, tall, tall, pl.BlockSpec((2, inner), lambda n, _: (0, 0))],
            out_specs=[out] * (2 * SIDE),
        ),
        out_shape=[shape] * (2 * SIDE),
        compiler_params=pltpu.CompilerParams(vmem_limit_bytes=60 * MIB),
        cost_estimate=pl.CostEstimate(
            flops=10 * query.size, bytes_accessed=12 * query.size, transcendentals=0
        ),
        name="prepare",
    )(place, query, key, value, qk_gain)


def attend_kernel(axes, place, gate_ref, _, *refs):
    held, arrived = refs[:SIDE], refs[SIDE : 2 * SIDE - 1]
    out, q_all, k_all, v_all, s_even, s_odd, m_even, m_odd, gates, result = refs[2 * SIDE - 1 :]
    frames, rows = held[0].shape[2:4]
    tokens = frames * rows
    length = SIDE * SIDE * tokens
    block, chunk = BLOCK, 512
    blocks = length // block
    scale = LOG2E / math.sqrt(HD)

    for i in range(SIDE):
        for j in range(SIDE):
            at = (i * SIDE + j) * tokens
            for kind, whole in enumerate((q_all, k_all, v_all)):
                part = held[i][0, kind] if j == 0 else arrived[j - 1][i, kind]
                whole[at : at + tokens, :HD] = part.reshape(tokens, HD)
    v_all[:, HD:] = jnp.ones((length, HD), jnp.bfloat16)
    for at in range(gates.shape[0] // rows):
        gates[at * rows : (at + 1) * rows, :] = jnp.broadcast_to(
            gate_ref[at % frames : at % frames + 1, :], (rows, HD)
        )

    def rows_of(n):
        at = n * block
        return pl.ds(at if isinstance(n, int) else pl.multiple_of(at, block), block)

    def step(following, s_next, m_next, current, s_now, m_now):
        if following is not None:
            q = q_all[rows_of(following), :]
            peak = None
        if current is not None:
            most = m_now[...] * scale
            total = None
        for at in range(0, length, chunk):
            if following is not None:
                scores = lax.dot_general(
                    q,
                    k_all[at : at + chunk, :],
                    (((1,), (1,)), ((), ())),
                    preferred_element_type=jnp.float32,
                )
                s_next[:, at : at + chunk] = scores
                for lane in range(0, chunk, HD):
                    part = scores[:, lane : lane + HD]
                    peak = part if peak is None else jnp.maximum(peak, part)
            if current is not None:
                weights = [
                    jnp.exp2(s_now[:, at + lane : at + lane + HD] * scale - most).astype(jnp.bfloat16)
                    for lane in range(0, chunk, HD)
                ]
                part = jnp.dot(
                    jnp.concatenate(weights, axis=1),
                    v_all[at : at + chunk, :],
                    preferred_element_type=jnp.float32,
                )
                total = part if total is None else total + part
        if following is not None:
            m_next[...] = jnp.broadcast_to(jnp.max(peak, axis=1, keepdims=True), (block, HD))
        if current is not None:
            attended = (total[:, :HD] / total[:, HD:]).astype(jnp.bfloat16).astype(jnp.float32)
            gate = gates[rows_of(current % (gates.shape[0] // block)), :]
            result[rows_of(current), :] = (gate * attended).astype(jnp.bfloat16)

    even, odd = (s_even, m_even), (s_odd, m_odd)
    step(0, *even, None, None, None)

    @pl.loop(0, blocks // 2 - 1)
    def _(pair):
        step(2 * pair + 1, *odd, 2 * pair, *even)
        step(2 * pair + 2, *even, 2 * pair + 1, *odd)

    step(blocks - 1, *odd, blocks - 2, *even)
    step(None, None, None, blocks - 1, *odd)
    for i in range(SIDE):
        for j in range(SIDE):
            at = (i * SIDE + j) * tokens
            source = index_of(place, axes, SIDE - i, SIDE - j)
            out[source] = result[at : at + tokens, :].reshape(frames, rows, HD)


def attend(axes, place, gate, before, held, arrived):
    frames, rows = held[0].shape[2:4]
    length = SIDE * SIDE * frames * rows
    block = BLOCK
    one = pl.BlockSpec((1, 3, frames, rows, HD), lambda n, _: (0, 0, 0, 0, 0))
    whole = pl.BlockSpec((SIDE, 3, frames, rows, HD), lambda n, _: (0, 0, 0, 0, 0))
    return pl.pallas_call(
        functools.partial(attend_kernel, axes),
        grid_spec=pltpu.PrefetchScalarGridSpec(
            num_scalar_prefetch=1,
            grid=(1,),
            in_specs=[pl.BlockSpec((frames, HD), lambda n, _: (0, 0)), pl.BlockSpec(memory_space=pl.ANY)]
            + [one] * SIDE
            + [whole] * (SIDE - 1),
            out_specs=pl.BlockSpec((SIDE * SIDE, frames, rows, HD), lambda n, _: (0, 0, 0, 0)),
            scratch_shapes=[
                pltpu.VMEM((length, HD), jnp.bfloat16),
                pltpu.VMEM((length, HD), jnp.bfloat16),
                pltpu.VMEM((length, 2 * HD), jnp.bfloat16),
                pltpu.VMEM((block, length), jnp.float32),
                pltpu.VMEM((block, length), jnp.float32),
                pltpu.VMEM((block, HD), jnp.float32),
                pltpu.VMEM((block, HD), jnp.float32),
                pltpu.VMEM((math.lcm(frames * rows, block), HD), jnp.float32),
                pltpu.VMEM((length, HD), jnp.bfloat16),
            ],
        ),
        out_shape=jax.ShapeDtypeStruct((SIDE * SIDE, frames, rows, HD), jnp.bfloat16),
        compiler_params=pltpu.CompilerParams(vmem_limit_bytes=60 * MIB),
        cost_estimate=pl.CostEstimate(
            flops=int(0.5 * length * length * HD) if axes[0] == "z" else 28 * length * length * HD, bytes_accessed=length if axes[0] == "z" else 8 * length * HD, transcendentals=0
        ),
        name="attend",
    )(place, gate, before, *held, *arrived)


def leaving_frame(slot, returned):
    return lax.dynamic_index_in_dim(returned, slot[0], 1, keepdims=False)


def assemble_kernel(*refs):
    *parts, out = refs
    for head, own in enumerate(parts):
        for group in range(own.shape[0]):
            at = (group * len(parts) + head) * HD
            out[:, :, at : at + HD] = own[group]


def assemble(parts):
    groups, frames, rows, _ = parts[0].shape
    inner = groups * len(parts) * HD
    step = 2
    own = pl.BlockSpec((groups, step, rows, HD), lambda n: (0, n, 0, 0))
    return pl.pallas_call(
        assemble_kernel,
        grid=(frames // step,),
        in_specs=[own] * len(parts),
        out_specs=pl.BlockSpec((step, rows, inner), lambda n: (n, 0, 0)),
        out_shape=jax.ShapeDtypeStruct((frames, rows, inner), jnp.bfloat16),
        compiler_params=pltpu.CompilerParams(vmem_limit_bytes=60 * MIB),
        cost_estimate=pl.CostEstimate(flops=0, bytes_accessed=4 * frames * rows * inner, transcendentals=0),
        name="assemble",
    )(*parts)


def hand_kernel(slot, place, *refs):
    *behind, fresh, _, out = refs

    @pl.when(place[2] != 0)
    def _():
        for head, part in enumerate(behind):
            for group in range(part.shape[0]):
                at = (group * len(behind) + head) * HD
                out[0, :, at : at + HD] = part[group]

    @pl.when(place[2] == 0)
    def _():
        out[0] = fresh[...]


def hand_over(slot, place, behind, fresh, gated):
    rows, inner = fresh.shape
    part = pl.BlockSpec(behind[0].shape, lambda n, *_: (0, 0, 0))
    return pl.pallas_call(
        hand_kernel,
        grid_spec=pltpu.PrefetchScalarGridSpec(
            num_scalar_prefetch=2,
            grid=(1,),
            in_specs=[part] * len(behind)
            + [pl.BlockSpec((rows, inner), lambda n, *_: (0, 0)), pl.BlockSpec(memory_space=pl.ANY)],
            out_specs=pl.BlockSpec((1, rows, inner), lambda n, slot, _: (slot[0], 0, 0)),
        ),
        out_shape=jax.ShapeDtypeStruct(gated.shape, gated.dtype),
        input_output_aliases={len(behind) + 3: 0},
        compiler_params=pltpu.CompilerParams(vmem_limit_bytes=60 * MIB),
        name="hand_over",
    )(slot, place, *behind, fresh, gated)


def level_gate(steps, gate_weight):
    half = gate_weight.shape[0] // 2
    freqs = jnp.exp(-math.log(10000.0) * jnp.arange(half, dtype=jnp.float32) / half)
    angles = steps.astype(jnp.float32)[:, None] * freqs[None, :]
    embed = jnp.concatenate([jnp.cos(angles), jnp.sin(angles)], axis=1).astype(jnp.bfloat16)
    return jnp.dot(embed, gate_weight, preferred_element_type=jnp.float32)


def shards(query, key, value, qk_gain, timesteps, gate_weight, slot, fresh):
    index = lax.axis_index("seq")
    section = lax.axis_index("section")
    place = jnp.stack([index // SIDE, index % SIDE, section]).astype(jnp.int32)
    columns = lax.dynamic_slice_in_dim(gate_weight, index * (2 * HD), 2 * HD, 1)
    gate = level_gate(timesteps, columns)
    prepared = prepare(place, query, key, value, qk_gain)
    ahead, back = list(prepared[:SIDE]), list(prepared[SIDE:])
    held = [None, first_stage(back, AXES[1][0])]
    ahead[2] = after(ahead[2], held[1][2])
    held[0] = first_stage(ahead, AXES[0][0])
    back_stacks = stacked(held[1])
    held[0][2] = after(held[0][2], *back_stacks)
    stacks = [stacked(held[0]), back_stacks]
    sections = lax.axis_size("section")
    parts, behind, before = [], [], qk_gain
    for head in range(2):
        arrived = second_stage(stacks[head], AXES[head][1])
        result = attend(AXES[head], place, gate[:, head * HD : (head + 1) * HD], before, held[head], arrived)
        before = result
        if parts:
            result = after(result, parts[0])
        returned = lax.all_to_all(result, "seq", split_axis=0, concat_axis=0, tiled=True)
        leaving = leaving_frame(slot, returned)
        behind.append(lax.ppermute(leaving, "section", [(n, n + 1) for n in range(sections - 1)]))
        parts.append(returned)
    return hand_over(slot, place, behind, fresh, assemble(parts))


def solution(mesh):
    placed = (
        P("section", "seq", None),
        P("section", "seq", None),
        P("section", "seq", None),
        P(),
        P("section"),
        P(),
        P(),
        P("seq", None),
    )
    return jax.shard_map(
        shards, mesh=mesh, in_specs=placed, out_specs=P("section", "seq", None), check_vma=False
    )
```

```python
import functools
import math

import jax
import jax.numpy as jnp
from jax import lax
from jax.experimental import pallas as pl
from jax.experimental.pallas import tpu as pltpu
from jax.sharding import PartitionSpec as P

HD = 128
SIDE = 4
LOG2E = 1.4426950408889634
MIB = 1024 * 1024
ATTEND_MIB = 60
BLOCK = 512


def moved(value, axis, steps):
    pairs = []
    for source in range(SIDE * SIDE):
        x, z = divmod(source, SIDE)
        if axis == "x":
            x = (x + steps) % SIDE
        else:
            z = (z + steps) % SIDE
        pairs.append((source, x * SIDE + z))
    return lax.ppermute(value, "seq", pairs)


def exchange(pieces, **groups):
    return lax.all_to_all(pieces, "seq", split_axis=0, concat_axis=0, tiled=True, **groups)


def first_stage(pieces, axis):
    return [pieces[0]] + [moved(pieces[i], axis, i) for i in range(1, SIDE)]


def stacked(held):
    return [jnp.stack([piece[j] for piece in held]) for j in range(1, SIDE)]


def second_stage(stacks, axis):
    return [moved(stack, axis, j + 1) for j, stack in enumerate(stacks)]


def after(value, *others):
    return lax.optimization_barrier((value, *others))[0]


def index_of(place, axes, i, j):
    steps = {axes[0]: i, axes[1]: j}
    return lax.rem(place[0] + steps["x"], SIDE) * SIDE + lax.rem(place[1] + steps["z"], SIDE)


def prepare_kernel(head, place, q_ref, k_ref, v_ref, gain_ref, *outs):
    inner = q_ref.shape[2]

    def factor_of(ref):
        total = None
        for at in range(0, inner, 512):
            part = ref[:, :, at : at + 512].astype(jnp.float32)
            part = part * part
            total = part if total is None else total + part
        mean = jnp.sum(total, axis=-1, keepdims=True) * (1.0 / inner)
        return lax.rsqrt(mean + 1e-06)

    q_factor, k_factor = factor_of(q_ref), factor_of(k_ref)
    for i in range(SIDE):
        for j in range(SIDE):
            group = index_of(place, ("z", "x"), i, j)
            if head:
                group = lax.rem(place[0] + i, SIDE) * SIDE + j
            at = pl.multiple_of((group * 2 + head) * HD, HD)
            for kind, (ref, factor) in enumerate(((q_ref, q_factor), (k_ref, k_factor))):
                gain = gain_ref[kind : kind + 1, pl.ds(at, HD)]
                part = ref[:, :, pl.ds(at, HD)].astype(jnp.float32) * factor * gain[None]
                outs[i][j, kind] = part.astype(jnp.bfloat16)
            outs[i][j, 2] = v_ref[:, :, pl.ds(at, HD)]


def prepare(head, place, query, key, value, qk_gain):
    frames, rows, inner = query.shape
    step = 2
    tall = pl.BlockSpec((step, rows, inner), lambda n, _: (n, 0, 0))
    out = pl.BlockSpec((SIDE, 3, step, rows, HD), lambda n, _: (0, 0, n, 0, 0))
    shape = jax.ShapeDtypeStruct((SIDE, 3, frames, rows, HD), jnp.bfloat16)
    return pl.pallas_call(
        functools.partial(prepare_kernel, head),
        grid_spec=pltpu.PrefetchScalarGridSpec(
            num_scalar_prefetch=1,
            grid=(frames // step,),
            in_specs=[tall, tall, tall, pl.BlockSpec((2, inner), lambda n, _: (0, 0))],
            out_specs=[out] * SIDE,
        ),
        out_shape=[shape] * SIDE,
        compiler_params=pltpu.CompilerParams(vmem_limit_bytes=60 * MIB),
        cost_estimate=pl.CostEstimate(
            flops=10 * query.size, bytes_accessed=12 * query.size, transcendentals=0
        ),
        name="prepare",
    )(place, query, key, value, qk_gain)


def attend_kernel(count, place, gate_ref, _, *refs):
    sent = refs[:count]
    out, q_all, k_all, v_all, s_even, s_odd, m_even, m_odd, gates, result = refs[count:]
    frames, rows = sent[0].shape[-3:-1]
    tokens = frames * rows
    length = SIDE * SIDE * tokens
    block, chunk = BLOCK, 512
    blocks = length // block
    scale = LOG2E / math.sqrt(HD)

    def part_of(n):
        i, j = divmod(n, SIDE)
        if count == 1:
            return sent[0], (i, j), lax.rem(place[0] + SIDE - j, SIDE) * SIDE + i
        source = index_of(place, ("z", "x"), SIDE - i, SIDE - j)
        return (sent[i], (0,), source) if j == 0 else (sent[SIDE + j - 1], (i,), source)

    for n in range(SIDE * SIDE):
        ref, index, _ = part_of(n)
        for kind, whole in enumerate((q_all, k_all, v_all)):
            whole[n * tokens : (n + 1) * tokens, :HD] = ref[(*index, kind)].reshape(tokens, HD)
    v_all[:, HD:] = jnp.ones((length, HD), jnp.bfloat16)
    for at in range(gates.shape[0] // rows):
        gates[at * rows : (at + 1) * rows, :] = jnp.broadcast_to(
            gate_ref[at % frames : at % frames + 1, :], (rows, HD)
        )

    def rows_of(n):
        at = n * block
        return pl.ds(at if isinstance(n, int) else pl.multiple_of(at, block), block)

    def step(following, s_next, m_next, current, s_now, m_now):
        if following is not None:
            q = q_all[rows_of(following), :]
            peak = None
        if current is not None:
            most = m_now[...] * scale
            total = None
        for at in range(0, length, chunk):
            if following is not None:
                scores = lax.dot_general(
                    q,
                    k_all[at : at + chunk, :],
                    (((1,), (1,)), ((), ())),
                    preferred_element_type=jnp.float32,
                )
                s_next[:, at : at + chunk] = scores
                for lane in range(0, chunk, HD):
                    part = scores[:, lane : lane + HD]
                    peak = part if peak is None else jnp.maximum(peak, part)
            if current is not None:
                weights = [
                    jnp.exp2(s_now[:, at + lane : at + lane + HD] * scale - most).astype(jnp.bfloat16)
                    for lane in range(0, chunk, HD)
                ]
                part = jnp.dot(
                    jnp.concatenate(weights, axis=1),
                    v_all[at : at + chunk, :],
                    preferred_element_type=jnp.float32,
                )
                total = part if total is None else total + part
        if following is not None:
            m_next[...] = jnp.broadcast_to(jnp.max(peak, axis=1, keepdims=True), (block, HD))
        if current is not None:
            attended = (total[:, :HD] / total[:, HD:]).astype(jnp.bfloat16).astype(jnp.float32)
            gate = gates[rows_of(current % (gates.shape[0] // block)), :]
            result[rows_of(current), :] = (gate * attended).astype(jnp.bfloat16)

    even, odd = (s_even, m_even), (s_odd, m_odd)
    step(0, *even, None, None, None)

    @pl.loop(0, blocks // 2 - 1)
    def _(pair):
        step(2 * pair + 1, *odd, 2 * pair, *even)
        step(2 * pair + 2, *even, 2 * pair + 1, *odd)

    step(blocks - 1, *odd, blocks - 2, *even)
    step(None, None, None, blocks - 1, *odd)
    for n in range(SIDE * SIDE):
        out[part_of(n)[2]] = result[n * tokens : (n + 1) * tokens, :].reshape(frames, rows, HD)


def attend(place, gate, before, *sent):
    frames, rows = sent[0].shape[-3:-1]
    length = SIDE * SIDE * frames * rows
    block = BLOCK
    one = pl.BlockSpec((1, 3, frames, rows, HD), lambda n, _: (0, 0, 0, 0, 0))
    whole = pl.BlockSpec((SIDE, 3, frames, rows, HD), lambda n, _: (0, 0, 0, 0, 0))
    every = pl.BlockSpec((SIDE, SIDE, 3, frames, rows, HD), lambda n, _: (0, 0, 0, 0, 0, 0))
    return pl.pallas_call(
        functools.partial(attend_kernel, len(sent)),
        grid_spec=pltpu.PrefetchScalarGridSpec(
            num_scalar_prefetch=1,
            grid=(1,),
            in_specs=[pl.BlockSpec((frames, HD), lambda n, _: (0, 0)), pl.BlockSpec(memory_space=pl.ANY)]
            + ([every] if len(sent) == 1 else [one] * SIDE + [whole] * (SIDE - 1)),
            out_specs=pl.BlockSpec((SIDE * SIDE, frames, rows, HD), lambda n, _: (0, 0, 0, 0)),
            scratch_shapes=[
                pltpu.VMEM((length, HD), jnp.bfloat16),
                pltpu.VMEM((length, HD), jnp.bfloat16),
                pltpu.VMEM((length, 2 * HD), jnp.bfloat16),
                pltpu.VMEM((block, length), jnp.float32),
                pltpu.VMEM((block, length), jnp.float32),
                pltpu.VMEM((block, HD), jnp.float32),
                pltpu.VMEM((block, HD), jnp.float32),
                pltpu.VMEM((math.lcm(frames * rows, block), HD), jnp.float32),
                pltpu.VMEM((length, HD), jnp.bfloat16),
            ],
        ),
        out_shape=jax.ShapeDtypeStruct((SIDE * SIDE, frames, rows, HD), jnp.bfloat16),
        compiler_params=pltpu.CompilerParams(vmem_limit_bytes=ATTEND_MIB * MIB),
        cost_estimate=pl.CostEstimate(
            flops=int(17 * length * length * HD) if len(sent) > 1 else 28 * length * length * HD, bytes_accessed=length if len(sent) > 1 else 8 * length * HD, transcendentals=0
        ),
        name="attend",
    )(place, gate, before, *sent)


def leaving_frame(slot, returned):
    return lax.dynamic_index_in_dim(returned, slot[0], 1, keepdims=False)


def assemble_kernel(*refs):
    *parts, out = refs
    for head, own in enumerate(parts):
        for group in range(own.shape[0]):
            at = (group * len(parts) + head) * HD
            out[:, :, at : at + HD] = own[group]


def assemble(parts):
    groups, frames, rows, _ = parts[0].shape
    inner = groups * len(parts) * HD
    step = 2
    own = pl.BlockSpec((groups, step, rows, HD), lambda n: (0, n, 0, 0))
    return pl.pallas_call(
        assemble_kernel,
        grid=(frames // step,),
        in_specs=[own] * len(parts),
        out_specs=pl.BlockSpec((step, rows, inner), lambda n: (n, 0, 0)),
        out_shape=jax.ShapeDtypeStruct((frames, rows, inner), jnp.bfloat16),
        compiler_params=pltpu.CompilerParams(vmem_limit_bytes=60 * MIB),
        cost_estimate=pl.CostEstimate(flops=0, bytes_accessed=4 * frames * rows * inner, transcendentals=0),
        name="assemble",
    )(*parts)


def hand_kernel(slot, place, *refs):
    *behind, fresh, _, out = refs

    @pl.when(place[2] != 0)
    def _():
        for head, part in enumerate(behind):
            for group in range(part.shape[0]):
                at = (group * len(behind) + head) * HD
                out[0, :, at : at + HD] = part[group]

    @pl.when(place[2] == 0)
    def _():
        out[0] = fresh[...]


def hand_over(slot, place, behind, fresh, gated):
    rows, inner = fresh.shape
    part = pl.BlockSpec(behind[0].shape, lambda n, *_: (0, 0, 0))
    return pl.pallas_call(
        hand_kernel,
        grid_spec=pltpu.PrefetchScalarGridSpec(
            num_scalar_prefetch=2,
            grid=(1,),
            in_specs=[part] * len(behind)
            + [pl.BlockSpec((rows, inner), lambda n, *_: (0, 0)), pl.BlockSpec(memory_space=pl.ANY)],
            out_specs=pl.BlockSpec((1, rows, inner), lambda n, slot, _: (slot[0], 0, 0)),
        ),
        out_shape=jax.ShapeDtypeStruct(gated.shape, gated.dtype),
        input_output_aliases={len(behind) + 3: 0},
        compiler_params=pltpu.CompilerParams(vmem_limit_bytes=60 * MIB),
        name="hand_over",
    )(slot, place, *behind, fresh, gated)


def level_gate(steps, gate_weight):
    half = gate_weight.shape[0] // 2
    freqs = jnp.exp(-math.log(10000.0) * jnp.arange(half, dtype=jnp.float32) / half)
    angles = steps.astype(jnp.float32)[:, None] * freqs[None, :]
    embed = jnp.concatenate([jnp.cos(angles), jnp.sin(angles)], axis=1).astype(jnp.bfloat16)
    return jnp.dot(embed, gate_weight, preferred_element_type=jnp.float32)


def shards(query, key, value, qk_gain, timesteps, gate_weight, slot, fresh):
    index = lax.axis_index("seq")
    section = lax.axis_index("section")
    place = jnp.stack([index // SIDE, index % SIDE, section]).astype(jnp.int32)
    columns = lax.dynamic_slice_in_dim(gate_weight, index * (2 * HD), 2 * HD, 1)
    gate = level_gate(timesteps, columns)
    ahead = list(prepare(0, place, query, key, value, qk_gain))
    back = list(prepare(1, after(place, ahead[0]), query, key, value, qk_gain))
    back = first_stage(back, "x")
    ahead = first_stage(ahead, "z")
    columns_of_z = [[x * SIDE + z for z in range(SIDE)] for x in range(SIDE)]
    back[3] = after(back[3], ahead[1], ahead[3])
    direct = exchange(jnp.stack(back, axis=1), axis_index_groups=columns_of_z)
    sent = [*ahead, *second_stage(stacked(ahead), "x")]
    sections = lax.axis_size("section")
    parts, behind, before = [], [], qk_gain
    for head, operands in enumerate((sent, [direct])):
        before = attend(place, gate[:, head * HD : (head + 1) * HD], before, *operands)
        returned = exchange(after(before, *parts))
        leaving = leaving_frame(slot, returned)
        behind.append(lax.ppermute(leaving, "section", [(n, n + 1) for n in range(sections - 1)]))
        parts.append(returned)
    return hand_over(slot, place, behind, fresh, assemble(parts))


def solution(mesh):
    placed = (
        P("section", "seq", None),
        P("section", "seq", None),
        P("section", "seq", None),
        P(),
        P("section"),
        P(),
        P(),
        P("seq", None),
    )
    return jax.shard_map(
        shards, mesh=mesh, in_specs=placed, out_specs=P("section", "seq", None), check_vma=False
    )
```

```python
import functools
import math

import jax
import jax.numpy as jnp
from jax import lax
from jax.experimental import pallas as pl
from jax.experimental.pallas import tpu as pltpu
from jax.sharding import PartitionSpec as P

HD = 128
SIDE = 4
LOG2E = 1.4426950408889634
MIB = 1024 * 1024
ATTEND_MIB = 60
BLOCK = 512


def moved(value, axis, steps):
    pairs = []
    for source in range(SIDE * SIDE):
        x, z = divmod(source, SIDE)
        if axis == "x":
            x = (x + steps) % SIDE
        else:
            z = (z + steps) % SIDE
        pairs.append((source, x * SIDE + z))
    return lax.ppermute(value, "seq", pairs)


def exchange(pieces, **groups):
    return lax.all_to_all(pieces, "seq", split_axis=0, concat_axis=0, tiled=True, **groups)


def first_stage(pieces, axis):
    return [pieces[0]] + [moved(pieces[i], axis, i) for i in range(1, SIDE)]


def stacked(held):
    return [jnp.stack([piece[j] for piece in held]) for j in range(1, SIDE)]


def second_stage(stacks, axis):
    return [moved(stack, axis, j + 1) for j, stack in enumerate(stacks)]


def after(value, *others):
    return lax.optimization_barrier((value, *others))[0]


def index_of(place, axes, i, j):
    steps = {axes[0]: i, axes[1]: j}
    return lax.rem(place[0] + steps["x"], SIDE) * SIDE + lax.rem(place[1] + steps["z"], SIDE)


def prepare_kernel(head, place, q_ref, k_ref, v_ref, gain_ref, *outs):
    inner = q_ref.shape[2]

    def factor_of(ref):
        total = None
        for at in range(0, inner, 512):
            part = ref[:, :, at : at + 512].astype(jnp.float32)
            part = part * part
            total = part if total is None else total + part
        mean = jnp.sum(total, axis=-1, keepdims=True) * (1.0 / inner)
        return lax.rsqrt(mean + 1e-06)

    q_factor, k_factor = factor_of(q_ref), factor_of(k_ref)
    for i in range(SIDE):
        for j in range(SIDE):
            group = index_of(place, ("z", "x"), i, j)
            if head:
                group = lax.rem(place[0] + i, SIDE) * SIDE + j
            at = pl.multiple_of((group * 2 + head) * HD, HD)
            for kind, (ref, factor) in enumerate(((q_ref, q_factor), (k_ref, k_factor))):
                gain = gain_ref[kind : kind + 1, pl.ds(at, HD)]
                part = ref[:, :, pl.ds(at, HD)].astype(jnp.float32) * factor * gain[None]
                outs[i][j, kind] = part.astype(jnp.bfloat16)
            outs[i][j, 2] = v_ref[:, :, pl.ds(at, HD)]


def prepare(head, place, query, key, value, qk_gain):
    frames, rows, inner = query.shape
    step = 2
    tall = pl.BlockSpec((step, rows, inner), lambda n, _: (n, 0, 0))
    out = pl.BlockSpec((SIDE, 3, step, rows, HD), lambda n, _: (0, 0, n, 0, 0))
    shape = jax.ShapeDtypeStruct((SIDE, 3, frames, rows, HD), jnp.bfloat16)
    return pl.pallas_call(
        functools.partial(prepare_kernel, head),
        grid_spec=pltpu.PrefetchScalarGridSpec(
            num_scalar_prefetch=1,
            grid=(frames // step,),
            in_specs=[tall, tall, tall, pl.BlockSpec((2, inner), lambda n, _: (0, 0))],
            out_specs=[out] * SIDE,
        ),
        out_shape=[shape] * SIDE,
        compiler_params=pltpu.CompilerParams(vmem_limit_bytes=60 * MIB),
        cost_estimate=pl.CostEstimate(
            flops=10 * query.size, bytes_accessed=12 * query.size, transcendentals=0
        ),
        name="prepare",
    )(place, query, key, value, qk_gain)


def attend_kernel(count, slot, place, gate_ref, _, *refs):
    sent = refs[:count]
    out, leaving, q_all, k_all, v_all, s_even, s_odd, m_even, m_odd, gates, result = refs[count:]
    frames, rows = sent[0].shape[-3:-1]
    tokens = frames * rows
    length = SIDE * SIDE * tokens
    block, chunk = BLOCK, 512
    blocks = length // block
    scale = LOG2E / math.sqrt(HD)

    def part_of(n):
        i, j = divmod(n, SIDE)
        if count == 1:
            return sent[0], (i, j), lax.rem(place[0] + SIDE - j, SIDE) * SIDE + i
        source = index_of(place, ("z", "x"), SIDE - i, SIDE - j)
        return (sent[i], (0,), source) if j == 0 else (sent[SIDE + j - 1], (i,), source)

    for n in range(SIDE * SIDE):
        ref, index, _ = part_of(n)
        for kind, whole in enumerate((q_all, k_all, v_all)):
            whole[n * tokens : (n + 1) * tokens, :HD] = ref[(*index, kind)].reshape(tokens, HD)
    v_all[:, HD:] = jnp.ones((length, HD), jnp.bfloat16)
    for at in range(gates.shape[0] // rows):
        gates[at * rows : (at + 1) * rows, :] = jnp.broadcast_to(
            gate_ref[at % frames : at % frames + 1, :], (rows, HD)
        )

    def rows_of(n):
        at = n * block
        return pl.ds(at if isinstance(n, int) else pl.multiple_of(at, block), block)

    def step(following, s_next, m_next, current, s_now, m_now):
        if following is not None:
            q = q_all[rows_of(following), :]
            peak = None
        if current is not None:
            most = m_now[...] * scale
            total = None
        for at in range(0, length, chunk):
            if following is not None:
                scores = lax.dot_general(
                    q,
                    k_all[at : at + chunk, :],
                    (((1,), (1,)), ((), ())),
                    preferred_element_type=jnp.float32,
                )
                s_next[:, at : at + chunk] = scores
                for lane in range(0, chunk, HD):
                    part = scores[:, lane : lane + HD]
                    peak = part if peak is None else jnp.maximum(peak, part)
            if current is not None:
                weights = [
                    jnp.exp2(s_now[:, at + lane : at + lane + HD] * scale - most).astype(jnp.bfloat16)
                    for lane in range(0, chunk, HD)
                ]
                part = jnp.dot(
                    jnp.concatenate(weights, axis=1),
                    v_all[at : at + chunk, :],
                    preferred_element_type=jnp.float32,
                )
                total = part if total is None else total + part
        if following is not None:
            m_next[...] = jnp.broadcast_to(jnp.max(peak, axis=1, keepdims=True), (block, HD))
        if current is not None:
            attended = (total[:, :HD] / total[:, HD:]).astype(jnp.bfloat16).astype(jnp.float32)
            gate = gates[rows_of(current % (gates.shape[0] // block)), :]
            result[rows_of(current), :] = (gate * attended).astype(jnp.bfloat16)

    even, odd = (s_even, m_even), (s_odd, m_odd)
    step(0, *even, None, None, None)

    @pl.loop(0, blocks // 2 - 1)
    def _(pair):
        step(2 * pair + 1, *odd, 2 * pair, *even)
        step(2 * pair + 2, *even, 2 * pair + 1, *odd)

    step(blocks - 1, *odd, blocks - 2, *even)
    step(None, None, None, blocks - 1, *odd)
    for n in range(SIDE * SIDE):
        source = part_of(n)[2]
        out[source] = result[n * tokens : (n + 1) * tokens, :].reshape(frames, rows, HD)
        leaving[source] = out[source, slot[0]]


def attend(slot, place, gate, before, *sent):
    frames, rows = sent[0].shape[-3:-1]
    length = SIDE * SIDE * frames * rows
    block = BLOCK
    one = pl.BlockSpec((1, 3, frames, rows, HD), lambda n, *_: (0, 0, 0, 0, 0))
    whole = pl.BlockSpec((SIDE, 3, frames, rows, HD), lambda n, *_: (0, 0, 0, 0, 0))
    every = pl.BlockSpec((SIDE, SIDE, 3, frames, rows, HD), lambda n, *_: (0, 0, 0, 0, 0, 0))
    return pl.pallas_call(
        functools.partial(attend_kernel, len(sent)),
        grid_spec=pltpu.PrefetchScalarGridSpec(
            num_scalar_prefetch=2,
            grid=(1,),
            in_specs=[pl.BlockSpec((frames, HD), lambda n, *_: (0, 0)), pl.BlockSpec(memory_space=pl.ANY)]
            + ([every] if len(sent) == 1 else [one] * SIDE + [whole] * (SIDE - 1)),
            out_specs=[
                pl.BlockSpec((SIDE * SIDE, frames, rows, HD), lambda n, *_: (0, 0, 0, 0)),
                pl.BlockSpec((SIDE * SIDE, rows, HD), lambda n, *_: (0, 0, 0)),
            ],
            scratch_shapes=[
                pltpu.VMEM((length, HD), jnp.bfloat16),
                pltpu.VMEM((length, HD), jnp.bfloat16),
                pltpu.VMEM((length, 2 * HD), jnp.bfloat16),
                pltpu.VMEM((block, length), jnp.float32),
                pltpu.VMEM((block, length), jnp.float32),
                pltpu.VMEM((block, HD), jnp.float32),
                pltpu.VMEM((block, HD), jnp.float32),
                pltpu.VMEM((math.lcm(frames * rows, block), HD), jnp.float32),
                pltpu.VMEM((length, HD), jnp.bfloat16),
            ],
        ),
        out_shape=[
            jax.ShapeDtypeStruct((SIDE * SIDE, frames, rows, HD), jnp.bfloat16),
            jax.ShapeDtypeStruct((SIDE * SIDE, rows, HD), jnp.bfloat16),
        ],
        compiler_params=pltpu.CompilerParams(vmem_limit_bytes=ATTEND_MIB * MIB),
        cost_estimate=pl.CostEstimate(
            flops=int(17 * length * length * HD) if len(sent) > 1 else 28 * length * length * HD, bytes_accessed=length if len(sent) > 1 else 8 * length * HD, transcendentals=0
        ),
        name="attend",
    )(slot, place, gate, before, *sent)


def hand_kernel(slot, behind, _, out):
    out[:, 0] = behind[...]


def hand_over(slot, behind, result):
    sources, rows, _ = behind.shape
    return pl.pallas_call(
        hand_kernel,
        grid_spec=pltpu.PrefetchScalarGridSpec(
            num_scalar_prefetch=1,
            grid=(1,),
            in_specs=[
                pl.BlockSpec(behind.shape, lambda n, _: (0, 0, 0)),
                pl.BlockSpec(memory_space=pl.ANY),
            ],
            out_specs=pl.BlockSpec((sources, 1, rows, HD), lambda n, slot: (0, slot[0], 0, 0)),
        ),
        out_shape=jax.ShapeDtypeStruct(result.shape, result.dtype),
        input_output_aliases={2: 0},
        compiler_params=pltpu.CompilerParams(vmem_limit_bytes=60 * MIB),
        name="hand_over",
    )(slot, behind, result)


def assemble_kernel(slot, place, *refs):
    *parts, fresh, out = refs
    step = out.shape[0]
    for n in range(step):
        new = jnp.logical_and(pl.program_id(0) * step + n == slot[0], place[2] == 0)

        @pl.when(jnp.logical_not(new))
        def _(n=n):
            for head, own in enumerate(parts):
                for group in range(own.shape[0]):
                    at = (group * len(parts) + head) * HD
                    out[n, :, at : at + HD] = own[group, n]

        @pl.when(new)
        def _(n=n):
            out[n] = fresh[...]


def assemble(slot, place, parts, fresh):
    groups, frames, rows, _ = parts[0].shape
    inner = fresh.shape[1]
    step = 2
    own = pl.BlockSpec((groups, step, rows, HD), lambda n, *_: (0, n, 0, 0))
    return pl.pallas_call(
        assemble_kernel,
        grid_spec=pltpu.PrefetchScalarGridSpec(
            num_scalar_prefetch=2,
            grid=(frames // step,),
            in_specs=[own] * len(parts) + [pl.BlockSpec((rows, inner), lambda n, *_: (0, 0))],
            out_specs=pl.BlockSpec((step, rows, inner), lambda n, *_: (n, 0, 0)),
        ),
        out_shape=jax.ShapeDtypeStruct((frames, rows, inner), jnp.bfloat16),
        compiler_params=pltpu.CompilerParams(vmem_limit_bytes=60 * MIB),
        cost_estimate=pl.CostEstimate(flops=0, bytes_accessed=4 * frames * rows * inner, transcendentals=0),
        name="assemble",
    )(slot, place, *parts, fresh)


def level_gate(steps, gate_weight):
    half = gate_weight.shape[0] // 2
    freqs = jnp.exp(-math.log(10000.0) * jnp.arange(half, dtype=jnp.float32) / half)
    angles = steps.astype(jnp.float32)[:, None] * freqs[None, :]
    embed = jnp.concatenate([jnp.cos(angles), jnp.sin(angles)], axis=1).astype(jnp.bfloat16)
    return jnp.dot(embed, gate_weight, preferred_element_type=jnp.float32)


def shards(query, key, value, qk_gain, timesteps, gate_weight, slot, fresh):
    index = lax.axis_index("seq")
    section = lax.axis_index("section")
    place = jnp.stack([index // SIDE, index % SIDE, section]).astype(jnp.int32)
    columns = lax.dynamic_slice_in_dim(gate_weight, index * (2 * HD), 2 * HD, 1)
    gate = level_gate(timesteps, columns)
    ahead = list(prepare(0, place, query, key, value, qk_gain))
    back = list(prepare(1, after(place, ahead[0]), query, key, value, qk_gain))
    back = first_stage(back, "x")
    ahead = first_stage(ahead, "z")
    columns_of_z = [[x * SIDE + z for z in range(SIDE)] for x in range(SIDE)]
    back[3] = after(back[3], ahead[1], ahead[3])
    direct = exchange(jnp.stack(back, axis=1), axis_index_groups=columns_of_z)
    sent = [*ahead, *second_stage(stacked(ahead), "x")]
    sections = lax.axis_size("section")
    parts, before = [], qk_gain
    for head, operands in enumerate((sent, [direct])):
        result, before = attend(slot, place, gate[:, head * HD : (head + 1) * HD], before, *operands)
        behind = lax.ppermute(before, "section", [(n, n + 1) for n in range(sections - 1)])
        parts.append(exchange(after(hand_over(slot, behind, result), *parts)))
    return assemble(slot, place, parts, fresh)


def solution(mesh):
    placed = (
        P("section", "seq", None),
        P("section", "seq", None),
        P("section", "seq", None),
        P(),
        P("section"),
        P(),
        P(),
        P("seq", None),
    )
    return jax.shard_map(
        shards, mesh=mesh, in_specs=placed, out_specs=P("section", "seq", None), check_vma=False
    )
```

```python
import functools
import math

import jax
import jax.numpy as jnp
from jax import lax
from jax.experimental import pallas as pl
from jax.experimental.pallas import tpu as pltpu
from jax.sharding import PartitionSpec as P

HD = 128
SIDE = 4
LOG2E = 1.4426950408889634
MIB = 1024 * 1024
ATTEND_MIB = 60
BLOCK = 512


def moved(value, axis, steps):
    pairs = []
    for source in range(SIDE * SIDE):
        x, z = divmod(source, SIDE)
        if axis == "x":
            x = (x + steps) % SIDE
        else:
            z = (z + steps) % SIDE
        pairs.append((source, x * SIDE + z))
    return lax.ppermute(value, "seq", pairs)


def exchange(pieces, **groups):
    return lax.all_to_all(pieces, "seq", split_axis=0, concat_axis=0, tiled=True, **groups)


def first_stage(pieces, axis):
    return [pieces[0]] + [moved(pieces[i], axis, i) for i in range(1, SIDE)]


def stacked(held):
    return [jnp.stack([piece[j] for piece in held]) for j in range(1, SIDE)]


def second_stage(stacks, axis):
    return [moved(stack, axis, j + 1) for j, stack in enumerate(stacks)]


def after(value, *others):
    return lax.optimization_barrier((value, *others))[0]


def index_of(place, axes, i, j):
    steps = {axes[0]: i, axes[1]: j}
    return lax.rem(place[0] + steps["x"], SIDE) * SIDE + lax.rem(place[1] + steps["z"], SIDE)


def prepare_kernel(head, place, q_ref, k_ref, v_ref, gain_ref, *outs):
    inner = q_ref.shape[2]

    def factor_of(ref):
        total = None
        for at in range(0, inner, 512):
            part = ref[:, :, at : at + 512].astype(jnp.float32)
            part = part * part
            total = part if total is None else total + part
        mean = jnp.sum(total, axis=-1, keepdims=True) * (1.0 / inner)
        return lax.rsqrt(mean + 1e-06)

    q_factor, k_factor = factor_of(q_ref), factor_of(k_ref)
    for i in range(SIDE):
        for j in range(SIDE):
            group = index_of(place, ("z", "x"), i, j)
            if head:
                group = lax.rem(place[0] + i, SIDE) * SIDE + j
            at = pl.multiple_of((group * 2 + head) * HD, HD)
            for kind, (ref, factor) in enumerate(((q_ref, q_factor), (k_ref, k_factor))):
                gain = gain_ref[kind : kind + 1, pl.ds(at, HD)]
                part = ref[:, :, pl.ds(at, HD)].astype(jnp.float32) * factor * gain[None]
                outs[i][j, kind] = part.astype(jnp.bfloat16)
            outs[i][j, 2] = v_ref[:, :, pl.ds(at, HD)]


def prepare(head, place, query, key, value, qk_gain):
    frames, rows, inner = query.shape
    step = 2
    tall = pl.BlockSpec((step, rows, inner), lambda n, _: (n, 0, 0))
    out = pl.BlockSpec((SIDE, 3, step, rows, HD), lambda n, _: (0, 0, n, 0, 0))
    shape = jax.ShapeDtypeStruct((SIDE, 3, frames, rows, HD), jnp.bfloat16)
    return pl.pallas_call(
        functools.partial(prepare_kernel, head),
        grid_spec=pltpu.PrefetchScalarGridSpec(
            num_scalar_prefetch=1,
            grid=(frames // step,),
            in_specs=[tall, tall, tall, pl.BlockSpec((2, inner), lambda n, _: (0, 0))],
            out_specs=[out] * SIDE,
        ),
        out_shape=[shape] * SIDE,
        compiler_params=pltpu.CompilerParams(vmem_limit_bytes=60 * MIB),
        cost_estimate=pl.CostEstimate(
            flops=10 * query.size, bytes_accessed=12 * query.size, transcendentals=0
        ),
        name="prepare",
    )(place, query, key, value, qk_gain)


def attend_kernel(count, place, gate_ref, _, *refs):
    sent = refs[:count]
    out, q_all, k_all, v_all, s_even, s_odd, m_even, m_odd, gates, result = refs[count:]
    frames, rows = sent[0].shape[-3:-1]
    tokens = frames * rows
    length = SIDE * SIDE * tokens
    block, chunk = BLOCK, 512
    blocks = length // block
    scale = LOG2E / math.sqrt(HD)

    def part_of(n):
        i, j = divmod(n, SIDE)
        if count == 1:
            return sent[0], (i, j), lax.rem(place[0] + SIDE - j, SIDE) * SIDE + i
        source = index_of(place, ("z", "x"), SIDE - i, SIDE - j)
        return (sent[i], (0,), source) if j == 0 else (sent[SIDE + j - 1], (i,), source)

    for n in range(SIDE * SIDE):
        ref, index, _ = part_of(n)
        for kind, whole in enumerate((q_all, k_all, v_all)):
            whole[n * tokens : (n + 1) * tokens, :HD] = ref[(*index, kind)].reshape(tokens, HD)
    v_all[:, HD:] = jnp.ones((length, HD), jnp.bfloat16)
    for at in range(gates.shape[0] // rows):
        gates[at * rows : (at + 1) * rows, :] = jnp.broadcast_to(
            gate_ref[at % frames : at % frames + 1, :], (rows, HD)
        )

    def rows_of(n):
        at = n * block
        return pl.ds(at if isinstance(n, int) else pl.multiple_of(at, block), block)

    def step(following, s_next, m_next, current, s_now, m_now):
        if following is not None:
            q = q_all[rows_of(following), :]
            peak = None
        if current is not None:
            most = m_now[...] * scale
            total = None
        for at in range(0, length, chunk):
            if following is not None:
                scores = lax.dot_general(
                    q,
                    k_all[at : at + chunk, :],
                    (((1,), (1,)), ((), ())),
                    preferred_element_type=jnp.float32,
                )
                s_next[:, at : at + chunk] = scores
                for lane in range(0, chunk, HD):
                    part = scores[:, lane : lane + HD]
                    peak = part if peak is None else jnp.maximum(peak, part)
            if current is not None:
                weights = [
                    jnp.exp2(s_now[:, at + lane : at + lane + HD] * scale - most).astype(jnp.bfloat16)
                    for lane in range(0, chunk, HD)
                ]
                part = jnp.dot(
                    jnp.concatenate(weights, axis=1),
                    v_all[at : at + chunk, :],
                    preferred_element_type=jnp.float32,
                )
                total = part if total is None else total + part
        if following is not None:
            m_next[...] = jnp.broadcast_to(jnp.max(peak, axis=1, keepdims=True), (block, HD))
        if current is not None:
            attended = (total[:, :HD] / total[:, HD:]).astype(jnp.bfloat16).astype(jnp.float32)
            gate = gates[rows_of(current % (gates.shape[0] // block)), :]
            result[rows_of(current), :] = (gate * attended).astype(jnp.bfloat16)

    even, odd = (s_even, m_even), (s_odd, m_odd)
    step(0, *even, None, None, None)

    @pl.loop(0, blocks // 2 - 1)
    def _(pair):
        step(2 * pair + 1, *odd, 2 * pair, *even)
        step(2 * pair + 2, *even, 2 * pair + 1, *odd)

    step(blocks - 1, *odd, blocks - 2, *even)
    step(None, None, None, blocks - 1, *odd)
    for n in range(SIDE * SIDE):
        out[part_of(n)[2]] = result[n * tokens : (n + 1) * tokens, :].reshape(frames, rows, HD)


def attend(place, gate, before, *sent):
    frames, rows = sent[0].shape[-3:-1]
    length = SIDE * SIDE * frames * rows
    block = BLOCK
    one = pl.BlockSpec((1, 3, frames, rows, HD), lambda n, _: (0, 0, 0, 0, 0))
    whole = pl.BlockSpec((SIDE, 3, frames, rows, HD), lambda n, _: (0, 0, 0, 0, 0))
    every = pl.BlockSpec((SIDE, SIDE, 3, frames, rows, HD), lambda n, _: (0, 0, 0, 0, 0, 0))
    return pl.pallas_call(
        functools.partial(attend_kernel, len(sent)),
        grid_spec=pltpu.PrefetchScalarGridSpec(
            num_scalar_prefetch=1,
            grid=(1,),
            in_specs=[pl.BlockSpec((frames, HD), lambda n, _: (0, 0)), pl.BlockSpec(memory_space=pl.ANY)]
            + ([every] if len(sent) == 1 else [one] * SIDE + [whole] * (SIDE - 1)),
            out_specs=pl.BlockSpec((SIDE * SIDE, frames, rows, HD), lambda n, _: (0, 0, 0, 0)),
            scratch_shapes=[
                pltpu.VMEM((length, HD), jnp.bfloat16),
                pltpu.VMEM((length, HD), jnp.bfloat16),
                pltpu.VMEM((length, 2 * HD), jnp.bfloat16),
                pltpu.VMEM((block, length), jnp.float32),
                pltpu.VMEM((block, length), jnp.float32),
                pltpu.VMEM((block, HD), jnp.float32),
                pltpu.VMEM((block, HD), jnp.float32),
                pltpu.VMEM((math.lcm(frames * rows, block), HD), jnp.float32),
                pltpu.VMEM((length, HD), jnp.bfloat16),
            ],
        ),
        out_shape=jax.ShapeDtypeStruct((SIDE * SIDE, frames, rows, HD), jnp.bfloat16),
        compiler_params=pltpu.CompilerParams(vmem_limit_bytes=ATTEND_MIB * MIB),
        cost_estimate=pl.CostEstimate(
            flops=int(17 * length * length * HD) if len(sent) > 1 else 28 * length * length * HD, bytes_accessed=length if len(sent) > 1 else 8 * length * HD, transcendentals=0
        ),
        name="attend",
    )(place, gate, before, *sent)


def leaving_frame(slot, returned):
    return lax.dynamic_index_in_dim(returned, slot[0], 1, keepdims=False)


def assemble_kernel(slot, place, *refs):
    fresh, out = refs[-2:]
    heads = (len(refs) - 2) // 2
    step = out.shape[0]
    for n in range(step):
        here = pl.program_id(0) * step + n == slot[0]

        def fill(pieces, n=n):
            for head, (own, index) in enumerate(pieces):
                for group in range(own.shape[0]):
                    at = (group * heads + head) * HD
                    out[n, :, at : at + HD] = own[(group, *index)]

        @pl.when(jnp.logical_not(here))
        def _(n=n, fill=fill):
            fill([(own, (n,)) for own in refs[:heads]])

        @pl.when(jnp.logical_and(here, place[2] != 0))
        def _(fill=fill):
            fill([(behind, ()) for behind in refs[heads : 2 * heads]])

        @pl.when(jnp.logical_and(here, place[2] == 0))
        def _(n=n):
            out[n] = fresh[...]


def assemble(slot, place, parts, behind, fresh):
    groups, frames, rows, _ = parts[0].shape
    inner = fresh.shape[1]
    step = 4
    own = pl.BlockSpec((groups, step, rows, HD), lambda n, *_: (0, n, 0, 0))
    frame = pl.BlockSpec((groups, rows, HD), lambda n, *_: (0, 0, 0))
    return pl.pallas_call(
        assemble_kernel,
        grid_spec=pltpu.PrefetchScalarGridSpec(
            num_scalar_prefetch=2,
            grid=(frames // step,),
            in_specs=[own] * len(parts)
            + [frame] * len(parts)
            + [pl.BlockSpec((rows, inner), lambda n, *_: (0, 0))],
            out_specs=pl.BlockSpec((step, rows, inner), lambda n, *_: (n, 0, 0)),
        ),
        out_shape=jax.ShapeDtypeStruct((frames, rows, inner), jnp.bfloat16),
        compiler_params=pltpu.CompilerParams(vmem_limit_bytes=60 * MIB),
        name="assemble",
    )(slot, place, *parts, *behind, fresh)


def level_gate(steps, gate_weight):
    half = gate_weight.shape[0] // 2
    freqs = jnp.exp(-math.log(10000.0) * jnp.arange(half, dtype=jnp.float32) / half)
    angles = steps.astype(jnp.float32)[:, None] * freqs[None, :]
    embed = jnp.concatenate([jnp.cos(angles), jnp.sin(angles)], axis=1).astype(jnp.bfloat16)
    return jnp.dot(embed, gate_weight, preferred_element_type=jnp.float32)


def shards(query, key, value, qk_gain, timesteps, gate_weight, slot, fresh):
    index = lax.axis_index("seq")
    section = lax.axis_index("section")
    place = jnp.stack([index // SIDE, index % SIDE, section]).astype(jnp.int32)
    columns = lax.dynamic_slice_in_dim(gate_weight, index * (2 * HD), 2 * HD, 1)
    gate = level_gate(timesteps, columns)
    ahead = list(prepare(0, place, query, key, value, qk_gain))
    back = list(prepare(1, after(place, ahead[0]), query, key, value, qk_gain))
    back = first_stage(back, "x")
    ahead = first_stage(ahead, "z")
    columns_of_z = [[x * SIDE + z for z in range(SIDE)] for x in range(SIDE)]
    back[3] = after(back[3], ahead[1], ahead[3])
    direct = exchange(jnp.stack(back, axis=1), axis_index_groups=columns_of_z)
    sent = [*ahead, *second_stage(stacked(ahead), "x")]
    sections = lax.axis_size("section")
    parts, behind, before = [], [], qk_gain
    for head, operands in enumerate((sent, [direct])):
        before = attend(place, gate[:, head * HD : (head + 1) * HD], before, *operands)
        returned = exchange(after(before, *parts))
        leaving = leaving_frame(slot, returned)
        behind.append(lax.ppermute(leaving, "section", [(n, n + 1) for n in range(sections - 1)]))
        parts.append(returned)
    return assemble(slot, place, parts, behind, fresh)


def solution(mesh):
    placed = (
        P("section", "seq", None),
        P("section", "seq", None),
        P("section", "seq", None),
        P(),
        P("section"),
        P(),
        P(),
        P("seq", None),
    )
    return jax.shard_map(
        shards, mesh=mesh, in_specs=placed, out_specs=P("section", "seq", None), check_vma=False
    )
```

```python
import functools
import math

import jax
import jax.numpy as jnp
from jax import lax
from jax.experimental import pallas as pl
from jax.experimental.pallas import tpu as pltpu
from jax.sharding import PartitionSpec as P

HD = 128
SIDE = 4
LOG2E = 1.4426950408889634
MIB = 1024 * 1024
ATTEND_MIB = 60
BLOCK = 512


def moved(value, axis, steps):
    pairs = []
    for source in range(SIDE * SIDE):
        x, z = divmod(source, SIDE)
        if axis == "x":
            x = (x + steps) % SIDE
        else:
            z = (z + steps) % SIDE
        pairs.append((source, x * SIDE + z))
    return lax.ppermute(value, "seq", pairs)


def exchange(pieces, **groups):
    return lax.all_to_all(pieces, "seq", split_axis=0, concat_axis=0, tiled=True, **groups)


def first_stage(pieces, axis):
    return [pieces[0]] + [moved(pieces[i], axis, i) for i in range(1, SIDE)]


def stacked(held):
    return [jnp.stack([piece[j] for piece in held]) for j in range(1, SIDE)]


def second_stage(stacks, axis):
    return [moved(stack, axis, j + 1) for j, stack in enumerate(stacks)]


def after(value, *others):
    return lax.optimization_barrier((value, *others))[0]


def index_of(place, axes, i, j):
    steps = {axes[0]: i, axes[1]: j}
    return lax.rem(place[0] + steps["x"], SIDE) * SIDE + lax.rem(place[1] + steps["z"], SIDE)


def prepare_kernel(head, place, q_ref, k_ref, v_ref, gain_ref, *outs):
    inner = q_ref.shape[2]

    def factor_of(ref):
        total = None
        for at in range(0, inner, 512):
            part = ref[:, :, at : at + 512].astype(jnp.float32)
            part = part * part
            total = part if total is None else total + part
        mean = jnp.sum(total, axis=-1, keepdims=True) * (1.0 / inner)
        return lax.rsqrt(mean + 1e-06)

    q_factor, k_factor = factor_of(q_ref), factor_of(k_ref)
    for i in range(SIDE):
        for j in range(SIDE):
            group = index_of(place, ("z", "x"), i, j)
            if head:
                group = lax.rem(place[0] + i, SIDE) * SIDE + j
            at = pl.multiple_of((group * 2 + head) * HD, HD)
            for kind, (ref, factor) in enumerate(((q_ref, q_factor), (k_ref, k_factor))):
                gain = gain_ref[kind : kind + 1, pl.ds(at, HD)]
                part = ref[:, :, pl.ds(at, HD)].astype(jnp.float32) * factor * gain[None]
                outs[i][j, kind] = part.astype(jnp.bfloat16)
            outs[i][j, 2] = v_ref[:, :, pl.ds(at, HD)]


def prepare(head, place, query, key, value, qk_gain):
    frames, rows, inner = query.shape
    step = 4
    tall = pl.BlockSpec((step, rows, inner), lambda n, _: (n, 0, 0))
    out = pl.BlockSpec((SIDE, 3, step, rows, HD), lambda n, _: (0, 0, n, 0, 0))
    shape = jax.ShapeDtypeStruct((SIDE, 3, frames, rows, HD), jnp.bfloat16)
    return pl.pallas_call(
        functools.partial(prepare_kernel, head),
        grid_spec=pltpu.PrefetchScalarGridSpec(
            num_scalar_prefetch=1,
            grid=(frames // step,),
            in_specs=[tall, tall, tall, pl.BlockSpec((2, inner), lambda n, _: (0, 0))],
            out_specs=[out] * SIDE,
        ),
        out_shape=[shape] * SIDE,
        compiler_params=pltpu.CompilerParams(vmem_limit_bytes=60 * MIB),
        cost_estimate=pl.CostEstimate(
            flops=10 * query.size, bytes_accessed=12 * query.size, transcendentals=0
        ),
        name="prepare",
    )(place, query, key, value, qk_gain)


def attend_kernel(count, place, gate_ref, _, *refs):
    sent = refs[:count]
    out, q_all, k_all, v_all, s_even, s_odd, m_even, m_odd, gates, result = refs[count:]
    frames, rows = sent[0].shape[-3:-1]
    tokens = frames * rows
    length = SIDE * SIDE * tokens
    block, chunk = BLOCK, 512
    blocks = length // block
    scale = LOG2E / math.sqrt(HD)

    def part_of(n):
        i, j = divmod(n, SIDE)
        if count == 1:
            return sent[0], (i, j), lax.rem(place[0] + SIDE - j, SIDE) * SIDE + i
        source = index_of(place, ("z", "x"), SIDE - i, SIDE - j)
        return (sent[i], (0,), source) if j == 0 else (sent[SIDE + j - 1], (i,), source)

    for n in range(SIDE * SIDE):
        ref, index, _ = part_of(n)
        for kind, whole in enumerate((q_all, k_all, v_all)):
            whole[n * tokens : (n + 1) * tokens, :HD] = ref[(*index, kind)].reshape(tokens, HD)
    v_all[:, HD:] = jnp.ones((length, HD), jnp.bfloat16)
    for at in range(gates.shape[0] // rows):
        gates[at * rows : (at + 1) * rows, :] = jnp.broadcast_to(
            gate_ref[at % frames : at % frames + 1, :], (rows, HD)
        )

    def rows_of(n):
        at = n * block
        return pl.ds(at if isinstance(n, int) else pl.multiple_of(at, block), block)

    def step(following, s_next, m_next, current, s_now, m_now):
        if following is not None:
            q = q_all[rows_of(following), :]
            peak = None
        if current is not None:
            most = m_now[...] * scale
            total = None
        for at in range(0, length, chunk):
            if following is not None:
                scores = lax.dot_general(
                    q,
                    k_all[at : at + chunk, :],
                    (((1,), (1,)), ((), ())),
                    preferred_element_type=jnp.float32,
                )
                s_next[:, at : at + chunk] = scores
                for lane in range(0, chunk, HD):
                    part = scores[:, lane : lane + HD]
                    peak = part if peak is None else jnp.maximum(peak, part)
            if current is not None:
                weights = [
                    jnp.exp2(s_now[:, at + lane : at + lane + HD] * scale - most).astype(jnp.bfloat16)
                    for lane in range(0, chunk, HD)
                ]
                part = jnp.dot(
                    jnp.concatenate(weights, axis=1),
                    v_all[at : at + chunk, :],
                    preferred_element_type=jnp.float32,
                )
                total = part if total is None else total + part
        if following is not None:
            m_next[...] = jnp.broadcast_to(jnp.max(peak, axis=1, keepdims=True), (block, HD))
        if current is not None:
            attended = (total[:, :HD] / total[:, HD:]).astype(jnp.bfloat16).astype(jnp.float32)
            gate = gates[rows_of(current % (gates.shape[0] // block)), :]
            result[rows_of(current), :] = (gate * attended).astype(jnp.bfloat16)

    even, odd = (s_even, m_even), (s_odd, m_odd)
    step(0, *even, None, None, None)

    @pl.loop(0, blocks // 2 - 1)
    def _(pair):
        step(2 * pair + 1, *odd, 2 * pair, *even)
        step(2 * pair + 2, *even, 2 * pair + 1, *odd)

    step(blocks - 1, *odd, blocks - 2, *even)
    step(None, None, None, blocks - 1, *odd)
    for n in range(SIDE * SIDE):
        out[part_of(n)[2]] = result[n * tokens : (n + 1) * tokens, :].reshape(frames, rows, HD)


def attend(place, gate, before, *sent):
    frames, rows = sent[0].shape[-3:-1]
    length = SIDE * SIDE * frames * rows
    block = BLOCK
    one = pl.BlockSpec((1, 3, frames, rows, HD), lambda n, _: (0, 0, 0, 0, 0))
    whole = pl.BlockSpec((SIDE, 3, frames, rows, HD), lambda n, _: (0, 0, 0, 0, 0))
    every = pl.BlockSpec((SIDE, SIDE, 3, frames, rows, HD), lambda n, _: (0, 0, 0, 0, 0, 0))
    return pl.pallas_call(
        functools.partial(attend_kernel, len(sent)),
        grid_spec=pltpu.PrefetchScalarGridSpec(
            num_scalar_prefetch=1,
            grid=(1,),
            in_specs=[pl.BlockSpec((frames, HD), lambda n, _: (0, 0)), pl.BlockSpec(memory_space=pl.ANY)]
            + ([every] if len(sent) == 1 else [one] * SIDE + [whole] * (SIDE - 1)),
            out_specs=pl.BlockSpec((SIDE * SIDE, frames, rows, HD), lambda n, _: (0, 0, 0, 0)),
            scratch_shapes=[
                pltpu.VMEM((length, HD), jnp.bfloat16),
                pltpu.VMEM((length, HD), jnp.bfloat16),
                pltpu.VMEM((length, 2 * HD), jnp.bfloat16),
                pltpu.VMEM((block, length), jnp.float32),
                pltpu.VMEM((block, length), jnp.float32),
                pltpu.VMEM((block, HD), jnp.float32),
                pltpu.VMEM((block, HD), jnp.float32),
                pltpu.VMEM((math.lcm(frames * rows, block), HD), jnp.float32),
                pltpu.VMEM((length, HD), jnp.bfloat16),
            ],
        ),
        out_shape=jax.ShapeDtypeStruct((SIDE * SIDE, frames, rows, HD), jnp.bfloat16),
        compiler_params=pltpu.CompilerParams(vmem_limit_bytes=ATTEND_MIB * MIB),
        cost_estimate=pl.CostEstimate(
            flops=int(17 * length * length * HD) if len(sent) > 1 else 28 * length * length * HD, bytes_accessed=length if len(sent) > 1 else 8 * length * HD, transcendentals=0
        ),
        name="attend",
    )(place, gate, before, *sent)


def leaving_frame(slot, returned):
    return lax.dynamic_index_in_dim(returned, slot[0], 1, keepdims=False)


def assemble_kernel(slot, place, *refs):
    fresh, out = refs[-2:]
    heads = (len(refs) - 2) // 2
    step = out.shape[0]
    for n in range(step):
        here = pl.program_id(0) * step + n == slot[0]

        def fill(pieces, n=n):
            for head, (own, index) in enumerate(pieces):
                for group in range(own.shape[0]):
                    at = (group * heads + head) * HD
                    out[n, :, at : at + HD] = own[(group, *index)]

        @pl.when(jnp.logical_not(here))
        def _(n=n, fill=fill):
            fill([(own, (n,)) for own in refs[:heads]])

        @pl.when(jnp.logical_and(here, place[2] != 0))
        def _(fill=fill):
            fill([(behind, ()) for behind in refs[heads : 2 * heads]])

        @pl.when(jnp.logical_and(here, place[2] == 0))
        def _(n=n):
            out[n] = fresh[...]


def assemble(slot, place, parts, behind, fresh):
    groups, frames, rows, _ = parts[0].shape
    inner = fresh.shape[1]
    step = 4
    own = pl.BlockSpec((groups, step, rows, HD), lambda n, *_: (0, n, 0, 0))
    frame = pl.BlockSpec((groups, rows, HD), lambda n, *_: (0, 0, 0))
    return pl.pallas_call(
        assemble_kernel,
        grid_spec=pltpu.PrefetchScalarGridSpec(
            num_scalar_prefetch=2,
            grid=(frames // step,),
            in_specs=[own] * len(parts)
            + [frame] * len(parts)
            + [pl.BlockSpec((rows, inner), lambda n, *_: (0, 0))],
            out_specs=pl.BlockSpec((step, rows, inner), lambda n, *_: (n, 0, 0)),
        ),
        out_shape=jax.ShapeDtypeStruct((frames, rows, inner), jnp.bfloat16),
        compiler_params=pltpu.CompilerParams(vmem_limit_bytes=60 * MIB),
        name="assemble",
    )(slot, place, *parts, *behind, fresh)


def level_gate(steps, gate_weight):
    half = gate_weight.shape[0] // 2
    freqs = jnp.exp(-math.log(10000.0) * jnp.arange(half, dtype=jnp.float32) / half)
    angles = steps.astype(jnp.float32)[:, None] * freqs[None, :]
    embed = jnp.concatenate([jnp.cos(angles), jnp.sin(angles)], axis=1).astype(jnp.bfloat16)
    return jnp.dot(embed, gate_weight, preferred_element_type=jnp.float32)


def shards(query, key, value, qk_gain, timesteps, gate_weight, slot, fresh):
    index = lax.axis_index("seq")
    section = lax.axis_index("section")
    place = jnp.stack([index // SIDE, index % SIDE, section]).astype(jnp.int32)
    columns = lax.dynamic_slice_in_dim(gate_weight, index * (2 * HD), 2 * HD, 1)
    gate = level_gate(timesteps, columns)
    ahead = list(prepare(0, place, query, key, value, qk_gain))
    back = list(prepare(1, after(place, ahead[0]), query, key, value, qk_gain))
    back = first_stage(back, "x")
    ahead = first_stage(ahead, "z")
    columns_of_z = [[x * SIDE + z for z in range(SIDE)] for x in range(SIDE)]
    back[3] = after(back[3], ahead[1], ahead[3])
    direct = exchange(jnp.stack(back, axis=1), axis_index_groups=columns_of_z)
    sent = [*ahead, *second_stage(stacked(ahead), "x")]
    sections = lax.axis_size("section")
    parts, behind, before = [], [], qk_gain
    for head, operands in enumerate((sent, [direct])):
        before = attend(place, gate[:, head * HD : (head + 1) * HD], before, *operands)
        returned = exchange(after(before, *parts))
        leaving = leaving_frame(slot, returned)
        behind.append(lax.ppermute(leaving, "section", [(n, n + 1) for n in range(sections - 1)]))
        parts.append(returned)
    return assemble(slot, place, parts, behind, fresh)


def solution(mesh):
    placed = (
        P("section", "seq", None),
        P("section", "seq", None),
        P("section", "seq", None),
        P(),
        P("section"),
        P(),
        P(),
        P("seq", None),
    )
    return jax.shard_map(
        shards, mesh=mesh, in_specs=placed, out_specs=P("section", "seq", None), check_vma=False
    )
```
